256 devices in a mesh: member: 4 (over z_hi), domain: 64 (over x, z_lo, y, core).
Axes of the slice: x: 4, y: 4, z: 8 (z_hi: 4, z_lo: 2; z = z_hi * 2 + z_lo), core: 2. Of those that a mesh axis runs over, the one named last changes fastest.
Arguments:
- positions: float32 [1024, 3, 128], P('domain'), may hold values from 0 to 8
- velocities: float32 [1024, 3, 128], P('domain'), may hold values from -3 to 3
- forces_old: float32 [1024, 3, 128], P('domain'), may hold values from -12 to 12
- species: int32 [1024, 128], P('domain'), may hold values from 0 to 2, as said below
- swap_lists: int32 [64, 3, 8], P('domain'), may hold values from 0 to 15, as said below
- ghost_lists: int32 [64, 64, 4], P('domain'), may hold values from -1 to 15, as said below
- pair_lists: int32 [256, 2, 128], P('domain'), may hold values from 0 to 34815, as said below
- tile_counts: int32 [64], P('domain'), may hold values from 2 to 4
- w_in: float32 [4, 8, 64], P('member'), may hold values from -2 to 2
- pair_embed: float32 [4, 4, 64], P('member'), may hold values from -4 to 4
- w_env: float32 [4, 2, 64, 64], P('member'), may hold values from -0.75 to 0.75
- w_mid: float32 [4, 2, 128, 64], P('member'), may hold values from -0.5 to 0.5
- w_out: float32 [4, 64, 64], P('member'), may hold values from -0.75 to 0.75
- w_last: float32 [4, 64], P('member'), may hold values from -0.75 to 0.75
Outputs:
- positions_new: float32 [1024, 3, 128], P('domain')
- velocities_new: float32 [1024, 3, 128], P('domain')
- forces_new: float32 [1024, 3, 128], P('domain')
The draws below stay inside these ranges and needn't reach their ends.
Inputs may be any that keep to these rules, and one draw needn't show every extreme that they name: `swap_lists`: within one domain and level the 8 bins are distinct. Domains sit on a periodic cube: the first coordinate of a domain is the Gray-decoded number whose bits, highest first, are index bits ..., 6, 3, 0; the second uses bits ..., 4, 1; the third ..., 5, 2. ghost_lists[p, d] names bins exactly when d differs from p and every coordinate differs by at most one, periodically; otherwise it is all -1. `pair_lists`: centres are below 2048; a neighbour differs from its centre; a neighbour at or above 2048 lies in a ghost slot whose ghost_lists entry toward this domain is not -1. `species`: present atoms of a bin fill its first slots.
All inputs are finite; a program needn't handle non-finite values.
Results may differ from the reference program's by a relative error of at most 0.0003.
Values sent between devices are 32-bit elements; how exact they have to be, the bound alone decides.
No kernel may reach another device: no remote copies, remote signals or barrier semaphores. Data moves between devices by JAX's collectives and lax.ppermute only.
A program may use at most 128 MiB of HBM per device.

```python
import math
import jax
import jax.numpy as jnp
import numpy as np
from jax import lax

CHANNELS = 64
NBASIS = 8
LAYERS = 2
MEMBERS = 4
BIN = 128
PAIR_TILE = 128
BINS_DEV = 16
GSLOT = 4
MOVE = 8
LEVELS = 3
TILES_DEV = 4
NBINS = 1024
OWN = 2048
TILES = 256
N_DOMAIN = 64


def domain_grid(domain_count):
    grid_depth = 0
    while 8 ** (grid_depth + 1) <= domain_count:
        grid_depth += 1
    placed = np.zeros((domain_count, 3), np.int64)
    for domain in range(domain_count):
        for coordinate in range(3):
            decoded = 0
            parity = 0
            for depth in range(grid_depth - 1, -1, -1):
                parity = parity ^ domain >> 3 * depth + coordinate & 1
                decoded = 2 * decoded + parity
            placed[domain, coordinate] = decoded
    return (placed, 2 ** grid_depth)


def beside_mask(domain_count):
    placed, side_count = domain_grid(domain_count)
    apart = (placed[:, None, :] - placed[None, :, :]) % side_count
    close = np.all((apart <= 1) | (apart == side_count - 1), axis=2)
    return close & (np.eye(domain_count) < 0.5)


def beside_table(domain_count):
    close = beside_mask(domain_count)
    listed = [[target for target in range(domain_count) if bool(close[source, target])] for source in range(domain_count)]
    return np.asarray(listed, dtype=np.int32)


def draw_species(key, part):
    key = jax.random.fold_in(key, 11)
    key_fill, key_kind = jax.random.split(key)
    bin_fill = jax.random.randint(key_fill, (NBINS, 1), 3 * BIN // 4, BIN + 1)
    kind_draw = jax.random.randint(key_kind, (NBINS, BIN), 0, 2)
    slot_index = jnp.arange(BIN, dtype=jnp.int32)[None, :]
    return jnp.where(slot_index < bin_fill, kind_draw, 2).astype(jnp.int32)


def draw_swap_lists(key, part):
    key = jax.random.fold_in(key, 23)
    scores = jax.random.randint(key, (N_DOMAIN, LEVELS, BINS_DEV), 0, 2 ** 20) * BINS_DEV
    scores = scores + jnp.arange(BINS_DEV, dtype=jnp.int32)
    ordering = jnp.argsort(scores, axis=-1)
    return ordering[:, :, :MOVE].astype(jnp.int32)


def draw_ghost_lists(key, part):
    key = jax.random.fold_in(key, 37)
    bin_pick = jax.random.randint(key, (N_DOMAIN, N_DOMAIN, GSLOT), 0, BINS_DEV)
    near_flag = jnp.asarray(beside_mask(N_DOMAIN))
    return jnp.where(near_flag[:, :, None], bin_pick, -1).astype(jnp.int32)


def draw_pair_lists(key, part):
    key = jax.random.fold_in(key, 41)
    key_centre, key_near, key_far, key_slot, key_flag = jax.random.split(key, 5)
    shape = (TILES, PAIR_TILE)
    centre = jax.random.randint(key_centre, shape, 0, OWN)
    near_index = jax.random.randint(key_near, shape, 0, OWN - 1)
    near_index = near_index + (near_index >= centre).astype(jnp.int32)
    near_table = jnp.asarray(beside_table(N_DOMAIN))
    far_pick = jax.random.randint(key_far, shape, 0, near_table.shape[1])
    tile_domain = (jnp.arange(TILES, dtype=jnp.int32) // TILES_DEV)[:, None]
    source_domain = near_table[tile_domain, far_pick]
    slot_pick = jax.random.randint(key_slot, shape, 0, GSLOT * BIN)
    far_index = OWN + source_domain * (GSLOT * BIN) + slot_pick
    local_flag = jax.random.randint(key_flag, shape, 0, 2)
    neighbour = jnp.where(local_flag == 1, near_index, far_index)
    return jnp.stack([centre, neighbour], axis=1).astype(jnp.int32)


def draw_tile_counts(key, part):
    key = jax.random.fold_in(key, 53)
    key_count, key_busy = jax.random.split(key)
    counts_drawn = jax.random.randint(key_count, (N_DOMAIN,), TILES_DEV // 2, TILES_DEV + 1)
    busiest = jax.random.randint(key_busy, (), 0, N_DOMAIN)
    return jnp.where(jnp.arange(N_DOMAIN, dtype=jnp.int32) == busiest, TILES_DEV, counts_drawn).astype(jnp.int32)


def levels(key, extent, cuts, low, high):
    gain = 1.0
    for position, shards_of in cuts:
        steps = jax.random.uniform(jax.random.fold_in(jax.random.fold_in(key, 6), position), (shards_of,), jnp.float32, low / len(cuts), high / len(cuts))
        gain = gain * jnp.repeat(jnp.exp(steps), extent[position] // shards_of).reshape((-1,) + (1,) * (len(extent) - 1 - position))
    return gain


def centred(rng, dims, scale, most, cuts=(), kind=jnp.bfloat16):
    result = scale * jax.random.normal(rng, dims, jnp.float32)
    if cuts:
        result = result * levels(rng, dims, cuts, -0.22, 0.18)
    return jnp.clip(result, -most, most).astype(kind)


def setup_inputs(seed: int = 0) -> dict:
    key_of = jax.random.split(jax.random.key(seed), 15)
    positions = jnp.clip(8.0 * jax.random.uniform(key_of[0], (NBINS, 3, BIN), jnp.float32) ** levels(key_of[0], (NBINS, 3, BIN), ((0, 64),), -0.2, 0.2), 0.0, 8.0)
    velocities = centred(key_of[1], (NBINS, 3, BIN), 0.5, 3.0, ((0, 64),), jnp.float32)
    forces_old = centred(key_of[2], (NBINS, 3, BIN), 2.0, 12.0, ((0, 64),), jnp.float32)
    species = draw_species(jax.random.fold_in(key_of[14], 71), 0)
    swap_lists = draw_swap_lists(jax.random.fold_in(key_of[14], 71), 0)
    ghost_lists = draw_ghost_lists(jax.random.fold_in(key_of[14], 71), 0)
    pair_lists = draw_pair_lists(jax.random.fold_in(key_of[14], 71), 0)
    tile_counts = draw_tile_counts(jax.random.fold_in(key_of[14], 71), 0)
    w_in = centred(key_of[8], (MEMBERS, NBASIS, CHANNELS), NBASIS ** -0.5, 2.0, ((0, 4),), jnp.float32)
    pair_embed = centred(key_of[9], (MEMBERS, 4, CHANNELS), 1.0, 4.0, ((0, 4),), jnp.float32)
    w_env = centred(key_of[10], (MEMBERS, LAYERS, CHANNELS, CHANNELS), CHANNELS ** -0.5, 0.75, ((0, 4),), jnp.float32)
    w_mid = centred(key_of[11], (MEMBERS, LAYERS, 2 * CHANNELS, CHANNELS), (2 * CHANNELS) ** -0.5, 0.5, ((0, 4),), jnp.float32)
    w_out = centred(key_of[12], (MEMBERS, CHANNELS, CHANNELS), CHANNELS ** -0.5, 0.75, ((0, 4),), jnp.float32)
    w_last = centred(key_of[13], (MEMBERS, CHANNELS), CHANNELS ** -0.5, 0.75, ((0, 4),), jnp.float32)
    return {"positions": positions, "velocities": velocities, "forces_old": forces_old, "species": species, "swap_lists": swap_lists, "ghost_lists": ghost_lists, "pair_lists": pair_lists, "tile_counts": tile_counts, "w_in": w_in, "pair_embed": pair_embed, "w_env": w_env, "w_mid": w_mid, "w_out": w_out, "w_last": w_last}


TIME_STEP = 0.1
SOFTENING = 0.5
CUTOFF = 6.0
MASS_HYDROGEN = 1.008
MASS_OXYGEN = 15.999
precise = lax.Precision.HIGHEST

def pair_energy(atom_table, kind_table, pair_block, tile_limit, weights, own_atoms):
    w_in, pair_embed, w_env, w_mid, w_out, w_last = weights
    centre = pair_block[:, 0, :].reshape(-1)
    neighbour = pair_block[:, 1, :].reshape(-1)
    tile_flag = jnp.arange(pair_block.shape[0], dtype=jnp.int32)[:, None] < tile_limit
    tile_live = jnp.broadcast_to(tile_flag, (pair_block.shape[0], pair_block.shape[2])).reshape(-1)
    kind_i = jnp.take(kind_table, centre)
    kind_j = jnp.take(kind_table, neighbour)
    offset = jnp.take(atom_table, neighbour, axis=1) - jnp.take(atom_table, centre, axis=1)
    distance = jnp.sqrt(lax.optimization_barrier(jnp.sum(offset * offset, axis=0)) + SOFTENING * SOFTENING)
    direction = offset / distance
    scaled = jnp.minimum(distance, CUTOFF) / CUTOFF
    envelope = 1.0 - 28.0 * scaled ** 6 + 48.0 * scaled ** 7 - 21.0 * scaled ** 8
    usable = (tile_live & (kind_i < 2) & (kind_j < 2) & (distance < CUTOFF)).astype(jnp.float32)
    frequency = jnp.arange(1, w_in.shape[0] + 1, dtype=jnp.float32) * (math.pi / CUTOFF)
    radial = math.sqrt(2.0 / CUTOFF) * jnp.sin(frequency[:, None] * distance[None, :]) / distance[None, :] * envelope[None, :]
    pair_kind = jnp.clip(2 * kind_i + kind_j, 0, 3)
    onehot = (pair_kind[None, :] == jnp.arange(4, dtype=jnp.int32)[:, None]).astype(jnp.float32)
    hidden = jax.nn.silu(jnp.einsum('bc,bp->cp', w_in, radial, precision=precise) + jnp.einsum('kc,kp->cp', pair_embed, onehot, precision=precise))
    channels = hidden.shape[0]
    for depth in range(w_env.shape[0]):
        weight = jnp.einsum('ic,ip->cp', w_env[depth], hidden, precision=precise)
        spread = direction[:, None, :] * (weight * usable[None, :])[None, :, :]
        environment = jnp.zeros((3, channels, own_atoms), jnp.float32).at[:, :, centre].add(spread)
        projected = lax.optimization_barrier(jnp.sum(direction[:, None, :] * jnp.take(environment, centre, axis=2), axis=0))
        joined = jnp.concatenate([hidden, weight * projected], axis=0)
        hidden = hidden + jax.nn.silu(jnp.einsum('ic,ip->cp', w_mid[depth], joined, precision=precise))
    readout = jnp.einsum('c,cp->p', w_last, jax.nn.silu(jnp.einsum('ic,ip->cp', w_out, hidden, precision=precise)), precision=precise)
    return jnp.sum(readout * envelope * usable)

def table_forces(atom_table, kind_table, pair_block, tile_limit, weights, own_atoms):

    def energy(coords):
        return pair_energy(coords, kind_table, pair_block, tile_limit, weights, own_atoms)
    value, pullback = jax.vjp(energy, atom_table)
    return -pullback(jnp.ones_like(value))[0]

def reference(positions, velocities, forces_old, species, swap_lists, ghost_lists, pair_lists, tile_counts, w_in, pair_embed, w_env, w_mid, w_out, w_last):
    domain_count = N_DOMAIN
    bin_count = BINS_DEV
    slot_count = BIN
    atom_state = jnp.concatenate([positions, velocities, forces_old], axis=1).reshape(domain_count, bin_count, 9, slot_count)
    kind_rows = species.reshape(domain_count, bin_count, slot_count)
    domains = jnp.arange(domain_count, dtype=jnp.int32)
    for level in range(LEVELS):
        partner = jnp.bitwise_xor(domains, 1 << level)
        swap_slots = swap_lists[:, level, :]
        outgoing = atom_state[domains[:, None], swap_slots]
        outgoing_kind = kind_rows[domains[:, None], swap_slots]
        atom_state = atom_state.at[domains[:, None], swap_slots].set(outgoing[partner])
        kind_rows = kind_rows.at[domains[:, None], swap_slots].set(outgoing_kind[partner])
    atom_mass = jnp.where(kind_rows == 1, MASS_OXYGEN, jnp.where(kind_rows == 0, MASS_HYDROGEN, 1.0)).astype(jnp.float32)[:, :, None, :]
    half_kick = atom_state[:, :, 3:6] + 0.5 * TIME_STEP * atom_state[:, :, 6:9] / atom_mass
    drifted = atom_state[:, :, 0:3] + TIME_STEP * half_kick
    ghost_dest = jnp.transpose(ghost_lists, (1, 0, 2))
    safe_slot = jnp.maximum(ghost_dest, 0)
    present = ghost_dest >= 0
    ghost_pos = jnp.where(present[..., None, None], drifted[domains[None, :, None], safe_slot], 0.0)
    ghost_kind = jnp.where(present[..., None], kind_rows[domains[None, :, None], safe_slot], 2)
    own_atoms = bin_count * slot_count
    weights = (w_in, pair_embed, w_env, w_mid, w_out, w_last)

    def one_domain(pieces):
        own_pos, own_kind, far_pos, far_kind, pair_block, tile_limit = pieces
        atom_table = jnp.concatenate([jnp.transpose(own_pos, (1, 0, 2)).reshape(3, -1), jnp.transpose(far_pos, (2, 0, 1, 3)).reshape(3, -1)], axis=1)
        kind_table = jnp.concatenate([own_kind.reshape(-1), far_kind.reshape(-1)])
        summed = jnp.zeros_like(atom_table)
        for member_index in range(MEMBERS):
            chosen = tuple((array[member_index] for array in weights))
            summed = summed + table_forces(atom_table, kind_table, pair_block, tile_limit, chosen, own_atoms)
        return summed
    all_forces = lax.map(one_domain, (drifted, kind_rows, ghost_pos, ghost_kind, pair_lists.reshape(domain_count, TILES_DEV, 2, PAIR_TILE), tile_counts))
    own_force = jnp.transpose(all_forces[:, :, :own_atoms].reshape(domain_count, 3, bin_count, slot_count), (0, 2, 1, 3))
    ghost_force = jnp.transpose(all_forces[:, :, own_atoms:].reshape(domain_count, 3, domain_count, GSLOT, slot_count), (0, 2, 3, 1, 4))
    selector = (ghost_lists[..., None] == jnp.arange(bin_count, dtype=jnp.int32)).astype(jnp.float32)
    returned = jnp.einsum('pdgb,dpgxa->pbxa', selector, ghost_force, precision=precise)
    forces_new = (own_force + returned) / MEMBERS
    velocities_new = half_kick + 0.5 * TIME_STEP * forces_new / atom_mass
    return (drifted.reshape(NBINS, 3, slot_count), velocities_new.reshape(NBINS, 3, slot_count), forces_new.reshape(NBINS, 3, slot_count))
```

```python
import functools
import math

import jax
import jax.numpy as jnp
from jax import lax
from jax.experimental import pallas as pl
from jax.experimental.pallas import tpu as pltpu
from jax.sharding import PartitionSpec as P

TIME_STEP = 0.1
SOFTENING = 0.5
CUTOFF = 6.0
MASS_HYDROGEN = 1.008
MASS_OXYGEN = 15.999

NDOM = 64
GROUP = 8
BINS = 16
LANES = 128
TILES = 4
PAIRS = TILES * LANES
OWN = BINS * LANES
CH = 64
NB = 8
LAYERS = 2
LEVELS = 3
MOVE = 8
GS = 4

SPEC = 3 * LANES
HALF = 4 * LANES
LIST = 7 * LANES
WIDE = 8 * LANES

F32 = jnp.float32
BF16 = jnp.bfloat16
I32 = jnp.int32

NEAR = []
for c2 in range(3):
    for c1 in range(3):
        for c0 in range(3):
            NEAR.append(
                (c0 & 1) | (c1 & 1) << 1 | (c2 & 1) << 2
                | (c0 >> 1) << 3 | (c1 >> 1) << 4 | (c2 >> 1) << 5
            )

VMEM = pl.BlockSpec(memory_space=pltpu.VMEM)
SMEM = pl.BlockSpec(memory_space=pltpu.SMEM)
PARAMS = pltpu.CompilerParams(vmem_limit_bytes=32 * 1024 * 1024)


def iota(shape, dim):
    return lax.broadcasted_iota(I32, shape, dim)


def dot(a, b, ca, cb):
    return lax.dot_general(a, b, (((ca,), (cb,)), ((), ())), preferred_element_type=F32)


def split2(x):
    hi = x.astype(BF16)
    return hi, (x - hi.astype(F32)).astype(BF16)


def split3(x):
    hi = x.astype(BF16)
    rest = x - hi.astype(F32)
    mid = rest.astype(BF16)
    return hi, mid, (rest - mid.astype(F32)).astype(BF16)


def mass_of(kind):
    return jnp.where(kind == 1.0, MASS_OXYGEN, jnp.where(kind == 0.0, MASS_HYDROGEN, 1.0))


def slot_of(low, high):
    drop0 = low >> 1
    drop1 = (low & 1) | ((low >> 2) << 1)
    drop2 = low & 3
    return jnp.where((high & 1) != 0, drop0, jnp.where((high & 2) != 0, drop1, drop2))


def pack_kernel(pos, vel, force, species, swap, ghost, out):
    kind = species[...].astype(F32)
    mass = mass_of(kind)
    listed = jnp.zeros((MOVE, LANES), F32)
    row = iota((MOVE, LANES), 0)
    lane = iota((MOVE, LANES), 1)
    for level in range(LEVELS):
        for k in range(MOVE):
            listed = jnp.where(
                (row == k) & (lane == level), swap[0, level, k].astype(F32), listed
            )
    drift = []
    half = []
    for x in range(3):
        kick = vel[:, x, :] + 0.5 * TIME_STEP * force[:, x, :] / mass
        half.append(kick)
        drift.append(pos[:, x, :] + TIME_STEP * kick)
    record = jnp.concatenate(drift + [kind] + half, axis=1)
    for e in range(GROUP):
        out[e, :, 0:LIST] = record
        out[e, 0:MOVE, LIST:WIDE] = listed
        out[e, MOVE:BINS, LIST:WIDE] = jnp.zeros((MOVE, LANES), F32)
        out[e, MOVE:BINS, LIST:LIST + GS] = ghost[0, pl.ds(e, GROUP, stride=GROUP), :].astype(F32)


def final_places(group):
    lane = iota((MOVE, LANES), 1)
    dom = lane // BINS
    own_bin = lane % BINS
    total = lane
    for level in reversed(range(LEVELS)):
        mine = jnp.zeros((MOVE, LANES), I32)
        for s in range(GROUP):
            column = group[s, 0:MOVE, LIST:WIDE][:, level:level + 1].astype(I32)
            mine = jnp.where(dom == s, column, mine)
        bit = 1 << level
        theirs = jnp.where(
            (dom & bit) != 0,
            pltpu.roll(mine, bit * BINS, 1),
            pltpu.roll(mine, LANES - bit * BINS, 1),
        )
        hit = mine == own_bin
        found = jnp.where(hit, (dom ^ bit) * BINS + theirs - lane, 0)
        source = lane + jnp.broadcast_to(jnp.sum(found, axis=0, keepdims=True), (MOVE, LANES))
        total = jnp.take_along_axis(source, total, axis=1)
    return total


def place_matrix(total):
    wide = jnp.broadcast_to(total[0:1, :], (LANES, LANES))
    return (iota((LANES, LANES), 0) == wide).astype(F32).astype(BF16)


def select_rows(chosen, data):
    hi, mid, lo = split3(data)
    return (dot(chosen, hi, 1, 0) + dot(chosen, mid, 1, 0)) + dot(chosen, lo, 1, 0)


def ghost_kernel(group, out, places):
    me = lax.axis_index("domain")
    low_me = me % GROUP
    high_me = me // GROUP
    total = final_places(group)
    places[...] = total
    matrix = place_matrix(total)
    lane = iota((GROUP, LANES), 1)
    high = iota((GROUP, LANES), 0) ^ high_me
    rows = [[jnp.zeros((GROUP, LANES), jnp.bool_) for _ in range(GS)] for _ in range(4)]
    for s in range(GROUP):
        low = s ^ low_me
        use = ((low & high) == 0) & (high != 0)
        slot = slot_of(low, high)
        lists = group[s, MOVE:BINS, LIST:WIDE].astype(I32)
        for g in range(GS):
            column = lists[:, g:g + 1]
            hit = (column + s * BINS == lane) & (column >= 0) & use
            for q in range(4):
                rows[q][g] = rows[q][g] | (hit & (slot == q))
    chosen = jnp.concatenate(
        [rows[q][g].astype(F32) for q in range(4) for g in range(GS)], axis=0
    ).astype(BF16)
    chosen = dot(chosen, matrix, 1, 1).astype(BF16)
    data = group[:, :, 0:HALF].reshape(GROUP * BINS, HALF)
    picked = select_rows(chosen, data)
    for r in range(4 * GS):
        out[:, r, :] = picked[r * GROUP:(r + 1) * GROUP, :]


def own_kernel(group, places, pos_new, rest):
    low_me = lax.axis_index("domain") % GROUP
    matrix = place_matrix(places[...])
    chosen = (iota((BINS, LANES), 1) == iota((BINS, LANES), 0) + low_me * BINS)
    chosen = dot(chosen.astype(F32).astype(BF16), matrix, 1, 1).astype(BF16)
    data = group[:, :, 0:LIST].reshape(GROUP * BINS, LIST)
    picked = select_rows(chosen, data)
    for x in range(3):
        pos_new[:, x, :] = picked[:, x * LANES:(x + 1) * LANES]
    rest[...] = picked[:, SPEC:LIST]


def take_row(table, index):
    parts = []
    for t in range(TILES):
        part = jnp.broadcast_to(index[:, t * LANES:(t + 1) * LANES], table.shape)
        parts.append(jnp.take_along_axis(table, part, axis=1)[0:1, :])
    return jnp.concatenate(parts, axis=1)


def pick(blocks, record, lane):
    columns = [[] for _ in range(4)]
    for t in range(TILES):
        cut = slice(t * LANES, (t + 1) * LANES)
        where_lane = jnp.broadcast_to(lane[:, cut], (8, LANES))
        where_bin = jnp.broadcast_to(record[:, cut], (8, LANES)) - iota((8, LANES), 0)
        sums = [jnp.zeros((8, LANES), F32) for _ in range(4)]
        for k, block in enumerate(blocks):
            hit = where_bin == 8 * k
            for x in range(4):
                got = jnp.take_along_axis(block(x), where_lane, axis=1)
                sums[x] = jnp.where(hit, got, sums[x])
        for x in range(4):
            columns[x].append(jnp.sum(sums[x], axis=0, keepdims=True))
    return [jnp.concatenate(c, axis=1) for c in columns]


def mm_t(weight, x):
    whi, wlo = split2(weight)
    xhi, xlo = split2(x)
    return dot(
        jnp.concatenate([whi, wlo, whi], axis=0), jnp.concatenate([xhi, xhi, xlo], axis=0), 0, 0
    )


def pieces(x):
    hi, lo = split2(x)
    return jnp.concatenate([hi, lo, hi, jnp.zeros(hi.shape, BF16)], axis=0)


def mm(weight, x):
    twice = jnp.concatenate([weight, weight], axis=1)
    whi = twice.astype(BF16)
    rest = twice - whi.astype(F32)
    wlo = jnp.where(iota(rest.shape, 1) < CH, rest, 0.0).astype(BF16)
    return dot(jnp.concatenate([whi, wlo], axis=1), x, 1, 0)


def sigmoid(x):
    return 1.0 / (1.0 + jnp.exp(-x))


def same_sum(parts, same):
    stacked = jnp.concatenate(parts, axis=0)
    hi, lo = split2(stacked)
    both = dot(jnp.concatenate([hi, lo], axis=0), same, 1, 0)
    n = stacked.shape[0]
    total = both[:n] + both[n:]
    return [total[x * CH:(x + 1) * CH] for x in range(3)]


def pair_rows(pairs, which):
    return jnp.concatenate([pairs[t, which:which + 1, :] for t in range(TILES)], axis=1)


def force_kernel(
    group, far, places, pairs, count, w_in, pair_embed, w_env, w_mid, w_out, w_last_col,
    out, first_weight,
):
    me = lax.axis_index("domain")
    low_me = me % GROUP
    high_me = me // GROUP
    total = places[...]
    centre = pair_rows(pairs, 0)
    neighbour = pair_rows(pairs, 1)

    lane8 = iota((GROUP, LANES), 1)
    listed = jnp.zeros((GROUP, LANES), I32)
    for s in range(GROUP):
        rows = group[s, MOVE:BINS, LIST:WIDE]
        rows = pltpu.roll(rows, s * BINS, 1) if s else rows
        listed = jnp.where(lane8 // BINS == s, rows.astype(I32), listed)
    listed = jnp.where(iota((GROUP, LANES), 0) == high_me, listed, 0)
    listed = jnp.broadcast_to(jnp.sum(listed, axis=0, keepdims=True), (GROUP, LANES))
    local_place = (lane8 // BINS) * BINS + jnp.maximum(listed, 0)
    local_total = jnp.take_along_axis(total, local_place, axis=1)

    centre_bin = take_row(total, low_me * BINS + (centre >> 7))
    centre_lane = centre & 127
    ghost = neighbour - OWN
    is_own = ghost < 0
    p = jnp.maximum(ghost, 0) >> 9
    g = (jnp.maximum(ghost, 0) >> 7) & 3
    p_low = p & 7
    p_high = p >> 3
    own_bin = take_row(total, low_me * BINS + jnp.where(is_own, neighbour >> 7, 0))
    local_bin = take_row(local_total, p_low * BINS + g)
    slot = slot_of(p_low ^ low_me, p_high ^ high_me) & 3
    far_bin = GROUP * BINS + p_high * BINS + slot * GS + g
    neighbour_bin = jnp.where(is_own, own_bin, jnp.where(p_high == high_me, local_bin, far_bin))
    neighbour_lane = neighbour & 127

    def piece(ref, s, half):
        return lambda x: ref[s, half * 8:(half + 1) * 8, x * LANES:(x + 1) * LANES]

    near_blocks = [piece(group, s, half) for s in range(GROUP) for half in range(2)]
    far_blocks = [piece(far, h, half) for h in range(GROUP) for half in range(2)]
    xi = pick(near_blocks, centre_bin, centre_lane)
    xj = pick(near_blocks + far_blocks, neighbour_bin, neighbour_lane)

    tile = iota((1, PAIRS), 1) // LANES
    delta = [xj[x] - xi[x] for x in range(3)]
    square = delta[0] * delta[0] + delta[1] * delta[1] + delta[2] * delta[2]
    r = jnp.sqrt(square + SOFTENING * SOFTENING)
    inverse = 1.0 / r
    unit = [delta[x] * inverse for x in range(3)]
    kind_i = xi[3].astype(I32)
    kind_j = xj[3].astype(I32)
    usable = (tile < count[0]) & (kind_i < 2) & (kind_j < 2) & (r < CUTOFF)
    live = usable.astype(F32)
    near = jnp.minimum(r, CUTOFF)
    s = near / CUTOFF
    s2 = s * s
    s5 = s2 * s2 * s
    s6 = s5 * s
    s7 = s6 * s
    u = 1.0 - 28.0 * s6 + 48.0 * s7 - 21.0 * s7 * s
    du = (-168.0 * s5 + 336.0 * s6 - 168.0 * s7) / CUTOFF
    wave = (iota((NB, PAIRS), 0) + 1).astype(F32) * (math.pi / CUTOFF)
    angle = wave * near
    sine = jnp.sin(angle)
    cosine = jnp.cos(angle)
    scale = math.sqrt(2.0 / CUTOFF)
    radial = scale * sine * inverse
    basis = radial * u
    dbasis = (scale * wave * cosine - radial) * inverse * u + radial * du

    rows = []
    for a in range(TILES):
        wide = jnp.broadcast_to(centre[:, a * LANES:(a + 1) * LANES].astype(F32), (LANES, LANES))
        column = jnp.transpose(wide)
        rows.append(
            jnp.concatenate(
                [
                    (column == centre[:, b * LANES:(b + 1) * LANES].astype(F32)).astype(F32)
                    for b in range(TILES)
                ],
                axis=1,
            ).astype(BF16)
        )
    same = jnp.concatenate(rows, axis=0)

    pair_kind = jnp.clip(2 * kind_i + kind_j, 0, 3)
    onehot = (iota((NB, PAIRS), 0) == pair_kind).astype(F32)
    first_weight[0:NB, :] = w_in[0]
    first_weight[NB:2 * NB, :] = jnp.zeros((NB, CH), F32)
    first_weight[NB:NB + 4, :] = pair_embed[0]
    weight0 = first_weight[...]
    pre0 = mm_t(weight0, jnp.concatenate([basis, onehot], axis=0))
    gate0 = sigmoid(pre0)
    h = pre0 * gate0
    saved = []
    for layer in range(LAYERS):
        w = mm_t(w_env[0, layer], h)
        live_w = w * live
        env = same_sum([live_w * unit[x] for x in range(3)], same)
        proj = unit[0] * env[0] + unit[1] * env[1] + unit[2] * env[2]
        pre = mm_t(w_mid[0, layer], jnp.concatenate([h, w * proj], axis=0))
        gate = sigmoid(pre)
        saved.append((w, live_w, env, proj, pre, gate))
        h = h + pre * gate
    z = mm_t(w_out[0], h)
    gate_z = sigmoid(z)
    last = w_last_col[...]
    readout = jnp.sum(last * (z * gate_z), axis=0, keepdims=True)

    def slope(pre, gate):
        return gate * (1.0 + pre * (1.0 - gate))

    dh = mm(w_out[0], pieces((last * (u * live)) * slope(z, gate_z)))
    dunit = [jnp.zeros((1, PAIRS), F32) for _ in range(3)]
    for layer in reversed(range(LAYERS)):
        w, live_w, env, proj, pre, gate = saved[layer]
        dpre = pieces(dh * slope(pre, gate))
        dq = mm(w_mid[0, layer, CH:2 * CH, :], dpre)
        dproj = dq * w
        dspread = same_sum([dproj * unit[x] for x in range(3)], same)
        back = unit[0] * dspread[0] + unit[1] * dspread[1] + unit[2] * dspread[2]
        dw = dq * proj + live * back
        for x in range(3):
            dunit[x] = dunit[x] + jnp.sum(
                dproj * env[x] + live_w * dspread[x], axis=0, keepdims=True
            )
        held = dh + mm(w_mid[0, layer, 0:CH, :], dpre)
        step = mm(w_env[0, layer], pieces(dw))
        dh = held + step
    slope0 = slope(pre0, gate0)
    dpre0 = held * slope0 + step * slope0
    grad_basis = mm(weight0, pieces(dpre0))[0:NB]
    dr = jnp.sum(grad_basis * dbasis, axis=0, keepdims=True) + readout * live * du
    along = dunit[0] * unit[0] + dunit[1] * unit[1] + dunit[2] * unit[2]
    radial_part = dr - along * inverse
    for x in range(3):
        out[x:x + 1, :] = jnp.where(usable, dunit[x] * inverse + unit[x] * radial_part, 0.0)
    out[3:4, :] = jnp.zeros((1, PAIRS), F32)


def spread_rows(ids, rows, grads, lane_row):
    mask = iota((rows, PAIRS), 0) == ids
    full = jnp.concatenate([jnp.where(mask, grads[x], 0.0) for x in range(3)], axis=0)
    hi, lo = split2(full)
    lanes = (iota((LANES, PAIRS), 0) == lane_row).astype(F32).astype(BF16)
    both = dot(jnp.concatenate([hi, lo], axis=0), lanes, 1, 1)
    both = both[:3 * rows] + both[3 * rows:]
    return [both[x * rows:(x + 1) * rows] for x in range(3)]


def scatter_kernel(f0, f1, f2, f3, pairs, out, own):
    me = lax.axis_index("domain")
    grad = (f0[...] + f2[...]) + (f1[...] + f3[...])
    grads = [grad[x:x + 1, :] for x in range(3)]
    centre = pair_rows(pairs, 0)
    neighbour = pair_rows(pairs, 1)
    ghost = jnp.maximum(neighbour - OWN, 0)
    apart = (ghost >> 9) ^ me
    code = jnp.zeros((1, PAIRS), I32)
    for k in range(3):
        code = code + 3 ** k * (((apart >> k) & 1) + 2 * ((apart >> (k + 3)) & 1))
    ids = jnp.where(neighbour < OWN, neighbour >> 7, BINS + (code - 1) * GS + ((ghost >> 7) & 3))
    far = spread_rows(ids, LANES, grads, neighbour & 127)
    near = spread_rows(centre >> 7, BINS, grads, centre & 127)
    out[...] = jnp.zeros(out.shape, F32)
    for x in range(3):
        own[x] = near[x] - far[x][0:BINS]
    for i, mask in enumerate(NEAR[1:]):
        p = me ^ mask
        start = BINS + i * GS
        for x in range(3):
            out[p, x * GS:(x + 1) * GS, :] = -far[x][start:start + GS]


def finish_kernel(returned, ghost, own, rest, vel_new, force_new):
    lane = iota((NDOM, BINS), 1)
    lists = ghost[0]
    chosen = jnp.concatenate(
        [(lists[:, g:g + 1] == lane).astype(F32) for g in range(GS)], axis=0
    ).astype(BF16)
    data = jnp.concatenate(
        [
            jnp.concatenate([returned[:, x * GS + g, :] for g in range(GS)], axis=0)
            for x in range(3)
        ],
        axis=1,
    )
    hi, lo = split2(data)
    added = dot(chosen, hi, 0, 0) + dot(chosen, lo, 0, 0)
    mass = mass_of(rest[:, 0:LANES])
    for x in range(3):
        force = (own[x] + added[:, x * LANES:(x + 1) * LANES]) * 0.25
        force_new[:, x, :] = force
        half = rest[:, (x + 1) * LANES:(x + 2) * LANES]
        vel_new[:, x, :] = half + 0.5 * TIME_STEP * force / mass


def call(kernel, name, shapes, args, specs=None, scratch=()):
    out = tuple(jax.ShapeDtypeStruct(s, d) for s, d in shapes)
    return pl.pallas_call(
        kernel,
        name=name,
        out_shape=out,
        in_specs=specs or [VMEM] * len(args),
        out_specs=tuple(VMEM for _ in out),
        scratch_shapes=list(scratch),
        compiler_params=PARAMS,
    )(*args)


LOW = [[g * GROUP + i for i in range(GROUP)] for g in range(GROUP)]
HIGH = [[g * GROUP + i for g in range(GROUP)] for i in range(GROUP)]


def on_device(
    positions, velocities, forces_old, species, swap_lists, ghost_lists, pair_lists, tile_counts,
    w_in, pair_embed, w_env, w_mid, w_out, w_last,
):
    (packed,) = call(
        pack_kernel, "pack", [((GROUP, BINS, WIDE), F32)],
        (positions, velocities, forces_old, species, swap_lists, ghost_lists),
        [VMEM, VMEM, VMEM, VMEM, SMEM, VMEM],
    )
    group = lax.all_to_all(packed, "domain", 0, 0, axis_index_groups=LOW, tiled=True)
    ghosts, places = call(
        ghost_kernel, "ghosts",
        [((GROUP, 4 * GS, HALF), F32), ((GROUP, LANES), I32)], (group,),
    )
    far = lax.all_to_all(ghosts, "domain", 0, 0, axis_index_groups=HIGH, tiled=True)
    pos_new, rest = call(
        own_kernel, "own", [((BINS, 3, LANES), F32), ((BINS, LIST - SPEC), F32)], (group, places)
    )
    (grad,) = call(
        force_kernel, "forces", [((4, PAIRS), F32)],
        (group, far, places, pair_lists, tile_counts, w_in, pair_embed, w_env, w_mid, w_out,
         w_last.reshape(CH, 1)),
        [VMEM, VMEM, VMEM, VMEM, SMEM, VMEM, VMEM, VMEM, VMEM, VMEM, VMEM],
        [pltpu.VMEM((2 * NB, CH), F32)],
    )
    others = [
        lax.ppermute(grad, "member", [(i, (i + s) % 4) for i in range(4)]) for s in (1, 2, 3)
    ]
    outgoing, own = call(
        scatter_kernel, "scatter",
        [((NDOM, 3 * GS, LANES), F32), ((3, BINS, LANES), F32)],
        (grad, *others, pair_lists),
    )
    returned = lax.all_to_all(outgoing, "domain", 0, 0, tiled=True)
    vel_new, force_new = call(
        finish_kernel, "finish",
        [((BINS, 3, LANES), F32), ((BINS, 3, LANES), F32)],
        (returned, ghost_lists, own, rest),
    )
    return pos_new, vel_new, force_new


def solution(mesh):
    return jax.shard_map(
        on_device,
        mesh=mesh,
        in_specs=(
            P("domain", None, None),
            P("domain", None, None),
            P("domain", None, None),
            P("domain", None),
            P("domain", None, None),
            P("domain", None, None),
            P("domain", None, None),
            P("domain"),
            P("member", None, None),
            P("member", None, None),
            P("member", None, None, None),
            P("member", None, None, None),
            P("member", None, None),
            P("member", None),
        ),
        out_specs=(P("domain", None, None), P("domain", None, None), P("domain", None, None)),
        check_vma=False,
    )
```

```python
import functools
import math

import jax
import jax.numpy as jnp
from jax import lax
from jax.experimental import pallas as pl
from jax.experimental.pallas import tpu as pltpu
from jax.sharding import PartitionSpec as P

TIME_STEP = 0.1
SOFTENING = 0.5
CUTOFF = 6.0
MASS_HYDROGEN = 1.008
MASS_OXYGEN = 15.999

NDOM = 64
GROUP = 8
BINS = 16
LANES = 128
TILES = 4
PAIRS = TILES * LANES
OWN = BINS * LANES
CH = 64
NB = 8
LAYERS = 2
LEVELS = 3
MOVE = 8
GS = 4


SPEC = 3 * LANES
HALF = 4 * LANES
LIST = 7 * LANES
WIDE = 8 * LANES

F32 = jnp.float32
BF16 = jnp.bfloat16
I32 = jnp.int32

NEAR = []
for c2 in range(3):
    for c1 in range(3):
        for c0 in range(3):
            NEAR.append(
                (c0 & 1) | (c1 & 1) << 1 | (c2 & 1) << 2
                | (c0 >> 1) << 3 | (c1 >> 1) << 4 | (c2 >> 1) << 5
            )

VMEM = pl.BlockSpec(memory_space=pltpu.VMEM)
SMEM = pl.BlockSpec(memory_space=pltpu.SMEM)
HBM = pl.BlockSpec(memory_space=pltpu.HBM)


def iota(shape, dim):
    return lax.broadcasted_iota(I32, shape, dim)


def dot(a, b, ca, cb):
    return lax.dot_general(a, b, (((ca,), (cb,)), ((), ())), preferred_element_type=F32)


def split2(x):
    hi = x.astype(BF16)
    return hi, (x - hi.astype(F32)).astype(BF16)


def split3(x):
    hi = x.astype(BF16)
    rest = x - hi.astype(F32)
    mid = rest.astype(BF16)
    return hi, mid, (rest - mid.astype(F32)).astype(BF16)


def mass_of(kind):
    return jnp.where(kind == 1.0, MASS_OXYGEN, jnp.where(kind == 0.0, MASS_HYDROGEN, 1.0))


def low_of(k, me):
    return (k >> 2) | (((k & 3) ^ ((me >> 1) & 3)) << 1)


def place_of(low, me):
    return (((low ^ me) & 1) << 2) | (low >> 1)


def record(group, k):
    return group[k // 4], k % 4


def lists_toward(group, k, me):
    ref, y = record(group, k)
    rows = ref[y, MOVE:BINS, LIST:WIDE]
    return jnp.where((me & 1) == 0, rows, pltpu.roll(rows, LANES - GS, 1)).astype(I32)


def table(group, start, stop):
    return jnp.concatenate(
        [ref[:, :, start:stop].reshape(4 * BINS, stop - start) for ref in group], axis=0
    )


def slot_of(low, high):
    drop0 = low >> 1
    drop1 = (low & 1) | ((low >> 2) << 1)
    drop2 = low & 3
    return jnp.where((high & 1) != 0, drop0, jnp.where((high & 2) != 0, drop1, drop2))


def start_kernel(*refs):
    count = 5
    sources = refs[:count]
    swap, out = refs[count:count + 2]
    copies = refs[count + 2:2 * count + 2]
    turned, sems = refs[2 * count + 2:]
    moves = [
        pltpu.make_async_copy(sources[i], copies[i], sems.at[i]) for i in range(count)
    ]
    for move in moves:
        move.start()
    pos, vel, force, species, ghost = copies

    listed = jnp.zeros((MOVE, LANES), F32)
    row = iota((MOVE, LANES), 0)
    lane = iota((MOVE, LANES), 1)
    for level in range(LEVELS):
        for k in range(MOVE):
            listed = jnp.where(
                (row == k) & (lane == level), swap[level, 0, k].astype(F32), listed
            )
    turned[...] = jnp.zeros((LANES, LANES), F32)
    for move in moves:
        move.wait()

    turned[0:GS, 0:NDOM] = ghost[0].astype(F32)
    turned[...] = jnp.transpose(turned[...])
    kind = species[...].astype(F32)
    mass = mass_of(kind)
    drift = []
    half = []
    for x in range(3):
        kick = vel[x] + 0.5 * TIME_STEP * force[x] / mass
        half.append(kick)
        drift.append(pos[x] + TIME_STEP * kick)
    packed = jnp.concatenate(drift + [kind] + half, axis=1)
    for y in range(4):
        out[y, :, 0:LIST] = packed
        out[y, 0:MOVE, LIST:WIDE] = listed
        toward = [turned[pl.ds(2 * y + core, GROUP, stride=GROUP), :] for core in range(2)]
        out[y, MOVE:BINS, LIST:WIDE] = toward[0] + pltpu.roll(toward[1], GS, 1)


def final_places(group):
    lane = iota((MOVE, LANES), 1)
    dom = lane // BINS
    own_bin = lane % BINS
    total = lane
    for level in reversed(range(LEVELS)):
        mine = jnp.zeros((MOVE, LANES), I32)
        for s in range(GROUP):
            ref, y = record(group, s)
            column = ref[y, 0:MOVE, LIST:WIDE][:, level:level + 1].astype(I32)
            mine = jnp.where(dom == s, column, mine)
        bit = (4, 1, 2)[level]
        theirs = jnp.where(
            (dom & bit) != 0,
            pltpu.roll(mine, bit * BINS, 1),
            pltpu.roll(mine, LANES - bit * BINS, 1),
        )
        hit = mine == own_bin
        found = jnp.where(hit, (dom ^ bit) * BINS + theirs - lane, 0)
        source = lane + jnp.broadcast_to(jnp.sum(found, axis=0, keepdims=True), (MOVE, LANES))
        total = jnp.take_along_axis(source, total, axis=1)
    return total


def place_matrix(total):
    wide = jnp.broadcast_to(total[0:1, :], (LANES, LANES))
    return (iota((LANES, LANES), 0) == wide).astype(F32).astype(BF16)


def select_rows(chosen, data):
    hi, mid, lo = split3(data)
    return (dot(chosen, hi, 1, 0) + dot(chosen, mid, 1, 0)) + dot(chosen, lo, 1, 0)


def ghost_kernel(near, other, out, places):
    group = (near, other)
    me = lax.axis_index("domain")
    high_me = me // GROUP
    total = final_places(group)
    places[...] = total
    matrix = place_matrix(total)
    lane = iota((GROUP, LANES), 1)
    high = iota((GROUP, LANES), 0) ^ high_me
    rows = [[jnp.zeros((GROUP, LANES), jnp.bool_) for _ in range(GS)] for _ in range(4)]
    for s in range(GROUP):
        low = low_of(s, me)
        use = ((low & high) == 0) & (high != 0)
        slot = slot_of(low, high)
        lists = lists_toward(group, s, me)
        for g in range(GS):
            column = lists[:, g:g + 1]
            hit = (column + s * BINS == lane) & (column >= 0) & use
            for q in range(4):
                rows[q][g] = rows[q][g] | (hit & (slot == q))
    chosen = jnp.concatenate(
        [rows[q][g].astype(F32) for q in range(4) for g in range(GS)], axis=0
    ).astype(BF16)
    chosen = dot(chosen, matrix, 1, 1).astype(BF16)
    picked = select_rows(chosen, table(group, 0, HALF))
    for r in range(4 * GS):
        out[:, r, :] = picked[r * GROUP:(r + 1) * GROUP, :]


def own_kernel(near, other, places, pos_new, kind, half):
    group = (near, other)
    place_me = (lax.axis_index("domain") >> 1) & 3
    matrix = place_matrix(places[...])
    chosen = (iota((BINS, LANES), 1) == iota((BINS, LANES), 0) + place_me * BINS)
    chosen = dot(chosen.astype(F32).astype(BF16), matrix, 1, 1).astype(BF16)
    picked = select_rows(chosen, table(group, 0, LIST))
    kind[...] = picked[:, SPEC:HALF]
    for x in range(3):
        pos_new[x] = picked[:, x * LANES:(x + 1) * LANES]
        half[x] = picked[:, HALF + x * LANES:HALF + (x + 1) * LANES]


def take_row(table, index):
    parts = []
    for t in range(TILES):
        part = jnp.broadcast_to(index[:, t * LANES:(t + 1) * LANES], table.shape)
        parts.append(jnp.take_along_axis(table, part, axis=1)[0:1, :])
    return jnp.concatenate(parts, axis=1)


def pick(blocks, record, lane):
    columns = [[] for _ in range(4)]
    for t in range(TILES):
        cut = slice(t * LANES, (t + 1) * LANES)
        where_lane = jnp.broadcast_to(lane[:, cut], (8, LANES))
        where_bin = jnp.broadcast_to(record[:, cut], (8, LANES)) - iota((8, LANES), 0)
        sums = [jnp.zeros((8, LANES), F32) for _ in range(4)]
        for k, block in enumerate(blocks):
            hit = where_bin == 8 * k
            for x in range(4):
                got = jnp.take_along_axis(block(x), where_lane, axis=1)
                sums[x] = jnp.where(hit, got, sums[x])
        for x in range(4):
            columns[x].append(jnp.sum(sums[x], axis=0, keepdims=True))
    return [jnp.concatenate(c, axis=1) for c in columns]


def three(x):
    hi, lo = split2(x)
    return jnp.concatenate([hi, hi, lo], axis=0)


def mm_t(weight, x):
    hi, lo = split2(weight)
    return dot(jnp.concatenate([hi, lo, hi], axis=0), x, 0, 0)


def mm(weight, x):
    hi, lo = split2(weight)
    return dot(jnp.concatenate([hi, lo, hi], axis=1), x, 1, 0)


def widen(x):
    return jnp.concatenate([x, jnp.zeros(x.shape, x.dtype)], axis=1)


def fill(x):
    return jnp.concatenate([x, jnp.zeros(x.shape, x.dtype)], axis=0)


def sigmoid(x):
    return 1.0 / (1.0 + jnp.exp(-x))


def same_sum(parts, same):
    high = []
    low = []
    for part in parts:
        hi, lo = split2(jnp.concatenate(part, axis=0))
        high.append(hi)
        low.append(lo)
    both = dot(jnp.concatenate(high + low, axis=0), same, 1, 0)
    n = 3 * CH
    result = []
    for m in range(len(parts)):
        total = both[m * n:(m + 1) * n] + both[(len(parts) + m) * n:(len(parts) + m + 1) * n]
        result.append([total[x * CH:(x + 1) * CH] for x in range(3)])
    return result


def pair_rows(pairs, which):
    return jnp.concatenate([pairs[t, which:which + 1, :] for t in range(TILES)], axis=1)


def force_kernel(
    near, other, far, places, pairs, count, w_in, pair_embed, w_env, w_mid_t, w_out, last_column,
    out, first_weight,
):
    group = (near, other)
    me = lax.axis_index("domain")
    low_me = me % GROUP
    high_me = me // GROUP
    place_me = low_me >> 1
    total = places[...]
    centre = pair_rows(pairs, 0)
    neighbour = pair_rows(pairs, 1)

    lane8 = iota((GROUP, LANES), 1)
    listed = jnp.zeros((GROUP, LANES), I32)
    for s in range(GROUP):
        rows = lists_toward(group, s, me)
        rows = pltpu.roll(rows, s * BINS, 1) if s else rows
        listed = jnp.where(lane8 // BINS == s, rows, listed)
    listed = jnp.where(iota((GROUP, LANES), 0) == high_me, listed, 0)
    listed = jnp.broadcast_to(jnp.sum(listed, axis=0, keepdims=True), (GROUP, LANES))
    local_place = (lane8 // BINS) * BINS + jnp.maximum(listed, 0)
    local_total = jnp.take_along_axis(total, local_place, axis=1)

    centre_bin = take_row(total, place_me * BINS + (centre >> 7))
    centre_lane = centre & 127
    ghost = neighbour - OWN
    is_own = ghost < 0
    p = jnp.maximum(ghost, 0) >> 9
    g = (jnp.maximum(ghost, 0) >> 7) & 3
    p_low = p & 7
    p_high = p >> 3
    own_bin = take_row(total, place_me * BINS + jnp.where(is_own, neighbour >> 7, 0))
    local_bin = take_row(local_total, place_of(p_low, me) * BINS + g)
    slot = slot_of(p_low ^ low_me, p_high ^ high_me) & 3
    far_bin = GROUP * BINS + p_high * BINS + slot * GS + g
    neighbour_bin = jnp.where(is_own, own_bin, jnp.where(p_high == high_me, local_bin, far_bin))
    neighbour_lane = neighbour & 127

    def piece(ref, s, half):
        return lambda x: ref[s, half * 8:(half + 1) * 8, x * LANES:(x + 1) * LANES]

    near_blocks = [piece(*record(group, s), half) for s in range(GROUP) for half in range(2)]
    far_blocks = [piece(far, h, half) for h in range(GROUP) for half in range(2)]
    xi = pick(near_blocks, centre_bin, centre_lane)
    xj = pick(near_blocks + far_blocks, neighbour_bin, neighbour_lane)

    tile = iota((1, PAIRS), 1) // LANES
    delta = [xj[x] - xi[x] for x in range(3)]
    square = delta[0] * delta[0] + delta[1] * delta[1] + delta[2] * delta[2]
    r = jnp.sqrt(square + SOFTENING * SOFTENING)
    inverse = 1.0 / r
    unit = [delta[x] * inverse for x in range(3)]
    kind_i = xi[3].astype(I32)
    kind_j = xj[3].astype(I32)
    usable = (tile < count[0]) & (kind_i < 2) & (kind_j < 2) & (r < CUTOFF)
    live = usable.astype(F32)
    short = jnp.minimum(r, CUTOFF)
    s = short / CUTOFF
    s2 = s * s
    s5 = s2 * s2 * s
    s6 = s5 * s
    s7 = s6 * s
    u = 1.0 - 28.0 * s6 + 48.0 * s7 - 21.0 * s7 * s
    du = (-168.0 * s5 + 336.0 * s6 - 168.0 * s7) / CUTOFF
    wave = (iota((NB, PAIRS), 0) + 1).astype(F32) * (math.pi / CUTOFF)
    angle = wave * short
    sine = jnp.sin(angle)
    cosine = jnp.cos(angle)
    scale = math.sqrt(2.0 / CUTOFF)
    radial = scale * sine * inverse
    basis = radial * u
    dbasis = (scale * wave * cosine - radial) * inverse * u + radial * du

    rows = []
    for a in range(TILES):
        wide = jnp.broadcast_to(centre[:, a * LANES:(a + 1) * LANES].astype(F32), (LANES, LANES))
        column = jnp.transpose(wide)
        rows.append(
            jnp.concatenate(
                [
                    (column == centre[:, b * LANES:(b + 1) * LANES].astype(F32)).astype(F32)
                    for b in range(TILES)
                ],
                axis=1,
            ).astype(BF16)
        )
    same = jnp.concatenate(rows, axis=0)

    pair_kind = jnp.clip(2 * kind_i + kind_j, 0, 3)
    onehot = (iota((NB, PAIRS), 0) == pair_kind).astype(F32)
    first = three(jnp.concatenate([basis, onehot], axis=0))
    every = range(1)
    first_weight[...] = jnp.zeros(first_weight.shape, F32)
    first_weight[0:NB, 0:CH] = w_in[0]
    first_weight[NB:NB + 4, 0:CH] = pair_embed[0]
    firsts = [first_weight[...]]
    envs = [[widen(w_env[0, layer]) for layer in range(LAYERS)]]
    mids = [[w_mid_t[0, layer] for layer in range(LAYERS)]]
    outs = [widen(w_out[0])]
    lasts = [last_column[...]]
    pre0 = [mm_t(firsts[m][:, 0:CH], first) for m in every]
    gate0 = [sigmoid(pre0[m]) for m in every]
    h = [pre0[m] * gate0[m] for m in every]
    saved = []
    for layer in range(LAYERS):
        w = [mm_t(envs[m][layer][:, 0:CH], three(h[m])) for m in every]
        live_w = [w[m] * live for m in every]
        env = same_sum([[live_w[m] * unit[x] for x in range(3)] for m in every], same)
        proj = [
            unit[0] * env[m][0] + unit[1] * env[m][1] + unit[2] * env[m][2] for m in every
        ]
        pre = [
            mm(mids[m][layer], three(jnp.concatenate([h[m], w[m] * proj[m]], axis=0)))
            for m in every
        ]
        gate = [sigmoid(pre[m]) for m in every]
        saved.append((w, live_w, env, proj, pre, gate))
        h = [h[m] + pre[m] * gate[m] for m in every]
    z = [mm_t(outs[m][:, 0:CH], three(h[m])) for m in every]
    gate_z = [sigmoid(z[m]) for m in every]
    readout = sum(
        jnp.sum(lasts[m] * (z[m] * gate_z[m]), axis=0, keepdims=True) for m in every
    )

    def slope(pre, gate):
        return gate * (1.0 + pre * (1.0 - gate))

    weight_z = u * live
    one = jnp.where(count[0] > -1, 1.0, 0.0)
    dh = [
        mm(outs[m], three(fill((lasts[m] * weight_z) * slope(z[m], gate_z[m]))))
        for m in every
    ]
    dunit = [jnp.zeros((1, PAIRS), F32) for _ in range(3)]
    for layer in reversed(range(LAYERS)):
        w, live_w, env, proj, pre, gate = saved[layer]
        djoined = [
            mm_t(mids[m][layer], three(dh[m] * slope(pre[m], gate[m]))) for m in every
        ]
        dq = [djoined[m][CH:] for m in every]
        dproj = [dq[m] * w[m] for m in every]
        dspread = same_sum([[dproj[m] * unit[x] for x in range(3)] for m in every], same)
        dw = []
        for m in every:
            back = unit[0] * dspread[m][0] + unit[1] * dspread[m][1] + unit[2] * dspread[m][2]
            dw.append(dq[m] * proj[m] + live * back)
        for x in range(3):
            dunit[x] = dunit[x] + jnp.sum(
                sum(dproj[m] * env[m][x] + live_w[m] * dspread[m][x] for m in every),
                axis=0, keepdims=True,
            )
        held = [dh[m] + one * djoined[m][:CH] for m in every]
        step = [mm(envs[m][layer], three(fill(dw[m]))) for m in every]
        if layer:
            dh = [held[m] + one * step[m] for m in every]
    grad_basis = jnp.zeros((NB, PAIRS), F32)
    for m in every:
        slope0 = slope(pre0[m], gate0[m])
        dpre0 = (held[m] + one * step[m]) * slope0
        grad_basis = grad_basis + one * mm(firsts[m], three(fill(dpre0)))[0:NB]
    dr = jnp.sum(grad_basis * dbasis, axis=0, keepdims=True) + readout * live * du
    along = dunit[0] * unit[0] + dunit[1] * unit[1] + dunit[2] * unit[2]
    radial_part = dr - along * inverse
    for x in range(3):
        out[x:x + 1, :] = jnp.where(usable, dunit[x] * inverse + unit[x] * radial_part, 0.0)
    out[3:4, :] = neighbour.astype(F32)


def spread_rows(ids, rows, grads, lane_row):
    mask = iota((rows, PAIRS), 0) == ids
    full = jnp.concatenate([jnp.where(mask, grads[x], 0.0) for x in range(3)], axis=0)
    hi, lo = split2(full)
    lanes = (iota((LANES, PAIRS), 0) == lane_row).astype(F32).astype(BF16)
    both = dot(jnp.concatenate([hi, lo], axis=0), lanes, 1, 1)
    both = both[:3 * rows] + both[3 * rows:]
    return [both[x * rows:(x + 1) * rows] for x in range(3)]


def ghost_code(neighbour, source):
    ghost = jnp.maximum(neighbour - OWN, 0)
    apart = (ghost >> 9) ^ source
    code = [((apart >> k) & 1) + 2 * ((apart >> (k + 3)) & 1) for k in range(3)]
    return code, (ghost >> 7) & 3


def scatter_kernel(grad, core_grad, pairs, out, own):
    me = lax.axis_index("domain")
    core = me & 1
    out[...] = jnp.zeros(out.shape, F32)

    centre = pair_rows(pairs, 0)
    neighbour = pair_rows(pairs, 1)
    code, g = ghost_code(neighbour, me)
    ids = BINS + ((code[0] >> 1) + 2 * code[1] + 6 * code[2] - 1) * GS + g
    ids = jnp.where(neighbour < OWN, neighbour >> 7, jnp.where(code[0] == 1, -1, ids))
    grads = [grad[x:x + 1, :] for x in range(3)]
    far = spread_rows(ids, 96, grads, neighbour & 127)
    near = spread_rows(centre >> 7, BINS, grads, centre & 127)
    for x in range(3):
        own[x] = near[x] - far[x][0:BINS]
    for i, mask in enumerate([mask for mask in NEAR if not mask & 1][1:]):
        start = BINS + i * GS
        for x in range(3):
            row = core * 3 * GS + x * GS
            out[(me ^ mask) >> 1, pl.ds(row, GS), :] = -far[x][start:start + GS]

    neighbour = (0.25 * core_grad[3:4, :]).astype(I32)
    code, g = ghost_code(neighbour, me ^ 1)
    ids = (code[1] + 3 * code[2]) * GS + g
    ids = jnp.where((neighbour < OWN) | (code[0] != 1), -1, ids)
    grads = [core_grad[x:x + 1, :] for x in range(3)]
    far = spread_rows(ids, 48, grads, neighbour & 127)
    for i, mask in enumerate([mask for mask in NEAR if mask & 1]):
        for x in range(3):
            row = (1 - core) * 3 * GS + x * GS
            out[(me ^ 1 ^ mask) >> 1, pl.ds(row, GS), :] = -far[x][i * GS:(i + 1) * GS]


def finish_kernel(returned, lists, own, kind, half, vel_new, force_new):
    chips = NDOM // 2
    chosen = jnp.concatenate(
        [
            (jnp.broadcast_to(lists[r:r + 1, :], (BINS, chips)) == iota((BINS, chips), 0)).astype(F32)
            for r in range(2 * GS)
        ],
        axis=1,
    ).astype(BF16)
    mass = mass_of(kind[...])
    for x in range(3):
        data = jnp.concatenate(
            [
                returned[:, core * 3 * GS + x * GS + g, :]
                for g in range(GS) for core in range(2)
            ],
            axis=0,
        )
        hi, lo = split2(data)
        added = dot(chosen, hi, 1, 0) + dot(chosen, lo, 1, 0)
        force = (own[x] + added) * 0.25
        force_new[x] = force
        vel_new[x] = half[x] + 0.5 * TIME_STEP * force / mass


def call(kernel, name, shapes, args, specs=None, scratch=(), limit=32):
    out = tuple(jax.ShapeDtypeStruct(s, d) for s, d in shapes)
    return pl.pallas_call(
        kernel,
        name=name,
        out_shape=out,
        in_specs=specs or [VMEM] * len(args),
        out_specs=tuple(VMEM for _ in out),
        scratch_shapes=list(scratch),
        compiler_params=pltpu.CompilerParams(vmem_limit_bytes=limit * 1024 * 1024),
    )(*args)


ALONG_Y = [[g * GROUP + c + 2 * i for i in range(4)] for g in range(GROUP) for c in range(2)]
HIGH = [[g * GROUP + i for g in range(GROUP)] for i in range(GROUP)]
CHIPS = [[2 * i + c for i in range(NDOM // 2)] for c in range(2)]


def other_core(x):
    return lax.ppermute(x, "domain", [(i, i ^ 1) for i in range(NDOM)])


def on_device(
    positions, velocities, forces_old, species, swap_lists, ghost_lists, pair_lists, tile_counts,
    w_in, pair_embed, w_env, w_mid, w_out, w_last,
):
    turn = lambda x: jnp.transpose(x, (1, 0, 2))
    ghosts_of = jnp.transpose(ghost_lists, (0, 2, 1))
    loads = (turn(positions), turn(velocities), turn(forces_old), species, ghosts_of)
    (packed,) = call(
        start_kernel, "start", [((4, BINS, WIDE), F32)],
        loads + (turn(swap_lists),),
        [HBM] * len(loads) + [SMEM],
        [pltpu.VMEM(x.shape, x.dtype) for x in loads]
        + [pltpu.VMEM((LANES, LANES), F32), pltpu.SemaphoreType.DMA((len(loads),))],
        limit=60,
    )
    near = lax.all_to_all(packed, "domain", 0, 0, axis_index_groups=ALONG_Y, tiled=True)
    other = other_core(near)
    ghosts, places = call(
        ghost_kernel, "ghosts",
        [((GROUP, 4 * GS, HALF), F32), ((GROUP, LANES), I32)], (near, other),
    )
    far = lax.all_to_all(ghosts, "domain", 0, 0, axis_index_groups=HIGH, tiled=True)
    (grad,) = call(
        force_kernel, "forces", [((4, PAIRS), F32)],
        (near, other, far, places, pair_lists, tile_counts, w_in, pair_embed, w_env,
         jnp.transpose(w_mid, (0, 1, 3, 2)), w_out, w_last.reshape(CH, 1)),
        [VMEM] * 5 + [SMEM] + [VMEM] * 6,
        [pltpu.VMEM((2 * NB, LANES), F32)],
    )
    grad = grad + lax.ppermute(grad, "member", [(i, i ^ 1) for i in range(4)])
    grad = grad + lax.ppermute(grad, "member", [(i, 3 - i) for i in range(4)])
    core_grad = other_core(grad)
    outgoing, own = call(
        scatter_kernel, "scatter",
        [((NDOM // 2, 6 * GS, LANES), F32), ((3, BINS, LANES), F32)],
        (grad, core_grad, pair_lists),
    )
    returned = lax.all_to_all(outgoing, "domain", 0, 0, axis_index_groups=CHIPS, tiled=True)
    pos_new, kind, half_new = call(
        own_kernel, "own",
        [((3, BINS, LANES), F32), ((BINS, LANES), F32), ((3, BINS, LANES), F32)],
        (near, other, places),
    )
    lists = ghost_lists[0].reshape(NDOM // 2, 2, GS).transpose(2, 1, 0).reshape(2 * GS, NDOM // 2)
    vel_new, force_new = call(
        finish_kernel, "finish",
        [((3, BINS, LANES), F32), ((3, BINS, LANES), F32)],
        (returned, lists, own, kind, half_new),
    )
    return turn(pos_new), turn(vel_new), turn(force_new)


def solution(mesh):
    return jax.shard_map(
        on_device,
        mesh=mesh,
        in_specs=(
            P("domain", None, None),
            P("domain", None, None),
            P("domain", None, None),
            P("domain", None),
            P("domain", None, None),
            P("domain", None, None),
            P("domain", None, None),
            P("domain"),
            P("member", None, None),
            P("member", None, None),
            P("member", None, None, None),
            P("member", None, None, None),
            P("member", None, None),
            P("member", None),
        ),
        out_specs=(P("domain", None, None), P("domain", None, None), P("domain", None, None)),
        check_vma=False,
    )
```

```python
import functools
import math

import jax
import jax.numpy as jnp
from jax import lax
from jax.experimental import pallas as pl
from jax.experimental.pallas import tpu as pltpu
from jax.sharding import PartitionSpec as P

TIME_STEP = 0.1
SOFTENING = 0.5
CUTOFF = 6.0
MASS_HYDROGEN = 1.008
MASS_OXYGEN = 15.999

NDOM = 64
GROUP = 8
BINS = 16
LANES = 128
TILES = 4
PAIRS = TILES * LANES
OWN = BINS * LANES
CH = 64
NB = 8
LAYERS = 2
LEVELS = 3
MOVE = 8
GS = 4


SPEC = 3 * LANES
HALF = 4 * LANES
LIST = 7 * LANES
WIDE = 8 * LANES

BACK = 6 * CH
FIRST = 10 * CH

F32 = jnp.float32
BF16 = jnp.bfloat16
I32 = jnp.int32

NEAR = []
for c2 in range(3):
    for c1 in range(3):
        for c0 in range(3):
            NEAR.append(
                (c0 & 1) | (c1 & 1) << 1 | (c2 & 1) << 2
                | (c0 >> 1) << 3 | (c1 >> 1) << 4 | (c2 >> 1) << 5
            )

VMEM = pl.BlockSpec(memory_space=pltpu.VMEM)
SMEM = pl.BlockSpec(memory_space=pltpu.SMEM)
HBM = pl.BlockSpec(memory_space=pltpu.HBM)


def iota(shape, dim):
    return lax.broadcasted_iota(I32, shape, dim)


def dot(a, b, ca, cb):
    return lax.dot_general(a, b, (((ca,), (cb,)), ((), ())), preferred_element_type=F32)


def split2(x):
    hi = x.astype(BF16)
    return hi, (x - hi.astype(F32)).astype(BF16)


def split3(x):
    hi = x.astype(BF16)
    rest = x - hi.astype(F32)
    mid = rest.astype(BF16)
    return hi, mid, (rest - mid.astype(F32)).astype(BF16)


def mass_of(kind):
    return jnp.where(kind == 1.0, MASS_OXYGEN, jnp.where(kind == 0.0, MASS_HYDROGEN, 1.0))


def low_of(k, me):
    return (k >> 2) | (((k & 3) ^ ((me >> 1) & 3)) << 1)


def place_of(low, me):
    return (((low ^ me) & 1) << 2) | (low >> 1)


def record(group, k):
    return group[k // 4], k % 4


def lists_toward(group, k, me):
    ref, y = record(group, k)
    rows = ref[y, MOVE:BINS, LIST:WIDE]
    return jnp.where((me & 1) == 0, rows, pltpu.roll(rows, LANES - GS, 1)).astype(I32)


def table(group, start, stop):
    return jnp.concatenate(
        [ref[:, :, start:stop].reshape(4 * BINS, stop - start) for ref in group], axis=0
    )


def slot_of(low, high):
    drop0 = low >> 1
    drop1 = (low & 1) | ((low >> 2) << 1)
    drop2 = low & 3
    return jnp.where((high & 1) != 0, drop0, jnp.where((high & 2) != 0, drop1, drop2))


def start_kernel(*refs):
    count = 5
    sources = refs[:count]
    swap, out = refs[count:count + 2]
    copies = refs[count + 2:2 * count + 2]
    turned, sems = refs[2 * count + 2:]
    moves = [
        pltpu.make_async_copy(sources[i], copies[i], sems.at[i]) for i in range(count)
    ]
    for move in moves:
        move.start()
    pos, vel, force, species, ghost = copies

    listed = jnp.zeros((MOVE, LANES), F32)
    row = iota((MOVE, LANES), 0)
    lane = iota((MOVE, LANES), 1)
    for level in range(LEVELS):
        for k in range(MOVE):
            listed = jnp.where(
                (row == k) & (lane == level), swap[level, 0, k].astype(F32), listed
            )
    turned[...] = jnp.zeros((LANES, LANES), F32)
    for move in moves:
        move.wait()

    turned[0:GS, 0:NDOM] = ghost[0].astype(F32)
    turned[...] = jnp.transpose(turned[...])
    kind = species[...].astype(F32)
    mass = mass_of(kind)
    drift = []
    half = []
    for x in range(3):
        kick = vel[x] + 0.5 * TIME_STEP * force[x] / mass
        half.append(kick)
        drift.append(pos[x] + TIME_STEP * kick)
    packed = jnp.concatenate(drift + [kind] + half, axis=1)
    for y in range(4):
        out[y, :, 0:LIST] = packed
        out[y, 0:MOVE, LIST:WIDE] = listed
        toward = [turned[pl.ds(2 * y + core, GROUP, stride=GROUP), :] for core in range(2)]
        out[y, MOVE:BINS, LIST:WIDE] = toward[0] + pltpu.roll(toward[1], GS, 1)


def final_places(group):
    lane = iota((MOVE, LANES), 1)
    dom = lane // BINS
    own_bin = lane % BINS
    total = lane
    for level in reversed(range(LEVELS)):
        mine = jnp.zeros((MOVE, LANES), I32)
        for s in range(GROUP):
            ref, y = record(group, s)
            column = ref[y, 0:MOVE, LIST:WIDE][:, level:level + 1].astype(I32)
            mine = jnp.where(dom == s, column, mine)
        bit = (4, 1, 2)[level]
        theirs = jnp.where(
            (dom & bit) != 0,
            pltpu.roll(mine, bit * BINS, 1),
            pltpu.roll(mine, LANES - bit * BINS, 1),
        )
        hit = mine == own_bin
        found = jnp.where(hit, (dom ^ bit) * BINS + theirs - lane, 0)
        source = lane + jnp.broadcast_to(jnp.sum(found, axis=0, keepdims=True), (MOVE, LANES))
        total = jnp.take_along_axis(source, total, axis=1)
    return total


def place_matrix(total):
    wide = jnp.broadcast_to(total[0:1, :], (LANES, LANES))
    return (iota((LANES, LANES), 0) == wide).astype(F32).astype(BF16)


def select_rows(chosen, data):
    hi, mid, lo = split3(data)
    return (dot(chosen, hi, 1, 0) + dot(chosen, mid, 1, 0)) + dot(chosen, lo, 1, 0)


def ghost_kernel(near, other, out, places):
    group = (near, other)
    me = lax.axis_index("domain")
    high_me = me // GROUP
    total = final_places(group)
    places[...] = total
    matrix = place_matrix(total)
    lane = iota((GROUP, LANES), 1)
    high = iota((GROUP, LANES), 0) ^ high_me
    rows = [[jnp.zeros((GROUP, LANES), jnp.bool_) for _ in range(GS)] for _ in range(4)]
    for s in range(GROUP):
        low = low_of(s, me)
        use = ((low & high) == 0) & (high != 0)
        slot = slot_of(low, high)
        lists = lists_toward(group, s, me)
        for g in range(GS):
            column = lists[:, g:g + 1]
            hit = (column + s * BINS == lane) & (column >= 0) & use
            for q in range(4):
                rows[q][g] = rows[q][g] | (hit & (slot == q))
    chosen = jnp.concatenate(
        [rows[q][g].astype(F32) for q in range(4) for g in range(GS)], axis=0
    ).astype(BF16)
    chosen = dot(chosen, matrix, 1, 1).astype(BF16)
    picked = select_rows(chosen, table(group, 0, HALF))
    for r in range(4 * GS):
        out[:, r, :] = picked[r * GROUP:(r + 1) * GROUP, :]


def own_kernel(near, other, places, pos_new, kind, half):
    group = (near, other)
    place_me = (lax.axis_index("domain") >> 1) & 3
    matrix = place_matrix(places[...])
    chosen = (iota((BINS, LANES), 1) == iota((BINS, LANES), 0) + place_me * BINS)
    chosen = dot(chosen.astype(F32).astype(BF16), matrix, 1, 1).astype(BF16)
    picked = select_rows(chosen, table(group, 0, LIST))
    kind[...] = picked[:, SPEC:HALF]
    for x in range(3):
        pos_new[x] = picked[:, x * LANES:(x + 1) * LANES]
        half[x] = picked[:, HALF + x * LANES:HALF + (x + 1) * LANES]


def take_row(table, index):
    parts = []
    for t in range(TILES):
        part = jnp.broadcast_to(index[:, t * LANES:(t + 1) * LANES], table.shape)
        parts.append(jnp.take_along_axis(table, part, axis=1)[0:1, :])
    return jnp.concatenate(parts, axis=1)


def pick(blocks, record, lane):
    columns = [[] for _ in range(4)]
    for t in range(TILES):
        cut = slice(t * LANES, (t + 1) * LANES)
        where_lane = jnp.broadcast_to(lane[:, cut], (8, LANES))
        where_bin = jnp.broadcast_to(record[:, cut], (8, LANES)) - iota((8, LANES), 0)
        sums = [jnp.zeros((8, LANES), F32) for _ in range(4)]
        for k, block in enumerate(blocks):
            hit = where_bin == 8 * k
            for x in range(4):
                got = jnp.take_along_axis(block(x), where_lane, axis=1)
                sums[x] = jnp.where(hit, got, sums[x])
        for x in range(4):
            columns[x].append(jnp.sum(sums[x], axis=0, keepdims=True))
    return [jnp.concatenate(c, axis=1) for c in columns]


def three(x):
    hi, lo = split2(x)
    return jnp.concatenate([hi, hi, lo], axis=0)


def mm_t(weight, x):
    hi, lo = split2(weight)
    return dot(jnp.concatenate([hi, lo, hi], axis=0), x, 0, 0)


def four(x):
    return jnp.concatenate([three(x), jnp.zeros(x.shape, BF16)], axis=0)


def left(weight):
    hi, lo = split2(weight)
    return jnp.concatenate([hi, lo, hi, jnp.zeros(hi.shape, BF16)], axis=1)


def turn_over(x):
    if x.shape[1] < LANES:
        x = jnp.concatenate([x, jnp.zeros((x.shape[0], LANES - x.shape[1]), F32)], axis=1)
    if x.shape[0] < LANES:
        x = jnp.concatenate([x, jnp.zeros((LANES - x.shape[0], LANES), F32)], axis=0)
    return jnp.transpose(x)


def sigmoid(x):
    return 1.0 / (1.0 + jnp.exp(-x))


def same_sum(parts, same):
    high = []
    low = []
    for part in parts:
        hi, lo = split2(jnp.concatenate(part, axis=0))
        high.append(hi)
        low.append(lo)
    both = dot(jnp.concatenate(high + low, axis=0), same, 1, 0)
    n = 3 * CH
    result = []
    for m in range(len(parts)):
        total = both[m * n:(m + 1) * n] + both[(len(parts) + m) * n:(len(parts) + m + 1) * n]
        result.append([total[x * CH:(x + 1) * CH] for x in range(3)])
    return result


def pair_rows(pairs, which):
    return jnp.concatenate([pairs[t, which:which + 1, :] for t in range(TILES)], axis=1)


def pair_kernel(
    near, other, places, pairs, w_in, pair_embed, w_env, w_mid_t, w_out,
    same, atoms, index, first, square, deep,
):
    first[...] = jnp.zeros(first.shape, F32)
    first[0:NB, 0:CH] = w_in[0]
    first[NB:NB + 4, 0:CH] = pair_embed[0]
    for k, weight in enumerate((w_env[0, 0], w_env[0, 1], w_out[0])):
        square[k * CH:(k + 1) * CH, :] = left(turn_over(weight)[0:CH, 0:CH])
        square[(3 + k) * CH:(4 + k) * CH, :] = left(weight)
    for layer in range(LAYERS):
        weight = w_mid_t[0, layer]
        start = BACK + layer * 2 * CH
        square[start:start + 2 * CH, :] = left(turn_over(weight)[:, 0:CH])
        hi, lo = split2(weight)
        deep[layer * CH:(layer + 1) * CH, :] = jnp.concatenate([hi, lo, hi], axis=1)
    square[FIRST:FIRST + 2 * NB, :] = left(first[:, 0:CH])

    group = (near, other)
    me = lax.axis_index("domain")
    low_me = me % GROUP
    high_me = me // GROUP
    place_me = low_me >> 1
    total = places[...]
    centre = pair_rows(pairs, 0)
    neighbour = pair_rows(pairs, 1)

    lane8 = iota((GROUP, LANES), 1)
    listed = jnp.zeros((GROUP, LANES), I32)
    for s in range(GROUP):
        rows = lists_toward(group, s, me)
        rows = pltpu.roll(rows, s * BINS, 1) if s else rows
        listed = jnp.where(lane8 // BINS == s, rows, listed)
    listed = jnp.where(iota((GROUP, LANES), 0) == high_me, listed, 0)
    listed = jnp.broadcast_to(jnp.sum(listed, axis=0, keepdims=True), (GROUP, LANES))
    local_place = (lane8 // BINS) * BINS + jnp.maximum(listed, 0)
    local_total = jnp.take_along_axis(total, local_place, axis=1)

    centre_bin = take_row(total, place_me * BINS + (centre >> 7))
    centre_lane = centre & 127
    ghost = neighbour - OWN
    is_own = ghost < 0
    p = jnp.maximum(ghost, 0) >> 9
    g = (jnp.maximum(ghost, 0) >> 7) & 3
    p_low = p & 7
    p_high = p >> 3
    own_bin = take_row(total, place_me * BINS + jnp.where(is_own, neighbour >> 7, 0))
    local_bin = take_row(local_total, place_of(p_low, me) * BINS + g)
    slot = slot_of(p_low ^ low_me, p_high ^ high_me) & 3
    is_far = (~is_own) & (p_high != high_me)
    near_bin = jnp.where(is_own, own_bin, jnp.where(is_far, -1, local_bin))
    neighbour_lane = neighbour & 127
    far_bin = jnp.where(is_far, p_high * BINS + slot * GS + g, -1)

    def piece(ref, s, half):
        return lambda x: ref[s, half * 8:(half + 1) * 8, x * LANES:(x + 1) * LANES]

    near_blocks = [piece(*record(group, s), half) for s in range(GROUP) for half in range(2)]
    xi = pick(near_blocks, centre_bin, centre_lane)
    xj = pick(near_blocks, near_bin, neighbour_lane)
    for x in range(4):
        atoms[x:x + 1, :] = xi[x]
        atoms[4 + x:5 + x, :] = xj[x]
    for r, values in enumerate((far_bin, neighbour_lane, neighbour)):
        index[r:r + 1, :] = values

    for a in range(TILES):
        wide = jnp.broadcast_to(centre[:, a * LANES:(a + 1) * LANES].astype(F32), (LANES, LANES))
        column = jnp.transpose(wide)
        same[a * LANES:(a + 1) * LANES, :] = (
            jnp.concatenate(
                [
                    (column == centre[:, b * LANES:(b + 1) * LANES].astype(F32)).astype(F32)
                    for b in range(TILES)
                ],
                axis=1,
            ).astype(BF16)
        )


def force_kernel(
    same_ref, atoms, index, far, count, first_weight, square, deep, last_column, out,
):
    def piece(h, half):
        return lambda x: far[h, half * 8:(half + 1) * 8, x * LANES:(x + 1) * LANES]

    same = same_ref[...]
    neighbour = index[2:3, :]
    blocks = [piece(h, half) for h in range(GROUP) for half in range(2)]
    xj = pick(blocks, index[0:1, :], index[1:2, :])
    xi = [atoms[x:x + 1, :] for x in range(4)]
    xj = [xj[x] + atoms[4 + x:5 + x, :] for x in range(4)]

    tile = iota((1, PAIRS), 1) // LANES
    delta = [xj[x] - xi[x] for x in range(3)]
    norm2 = delta[0] * delta[0] + delta[1] * delta[1] + delta[2] * delta[2]
    r = jnp.sqrt(norm2 + SOFTENING * SOFTENING)
    inverse = 1.0 / r
    unit = [delta[x] * inverse for x in range(3)]
    kind_i = xi[3].astype(I32)
    kind_j = xj[3].astype(I32)
    usable = (tile < count[0]) & (kind_i < 2) & (kind_j < 2) & (r < CUTOFF)
    live = usable.astype(F32)
    short = jnp.minimum(r, CUTOFF)
    s = short / CUTOFF
    s2 = s * s
    s5 = s2 * s2 * s
    s6 = s5 * s
    s7 = s6 * s
    u = 1.0 - 28.0 * s6 + 48.0 * s7 - 21.0 * s7 * s
    du = (-168.0 * s5 + 336.0 * s6 - 168.0 * s7) / CUTOFF
    wave = (iota((NB, PAIRS), 0) + 1).astype(F32) * (math.pi / CUTOFF)
    angle = wave * short
    sine = jnp.sin(angle)
    cosine = jnp.cos(angle)
    scale = math.sqrt(2.0 / CUTOFF)
    radial = scale * sine * inverse
    basis = radial * u
    dbasis = (scale * wave * cosine - radial) * inverse * u + radial * du

    pair_kind = jnp.clip(2 * kind_i + kind_j, 0, 3)
    onehot = (iota((NB, PAIRS), 0) == pair_kind).astype(F32)
    first = three(jnp.concatenate([basis, onehot], axis=0))
    every = range(1)

    def ready(k, rows=CH):
        return square[k * CH:k * CH + rows, :]

    lasts = [last_column[...]]
    pre0 = [mm_t(first_weight[:, 0:CH], first) for m in every]
    gate0 = [sigmoid(pre0[m]) for m in every]
    h = [pre0[m] * gate0[m] for m in every]
    saved = []
    for layer in range(LAYERS):
        w = [dot(ready(layer), four(h[m]), 1, 0) for m in every]
        live_w = [w[m] * live for m in every]
        env = same_sum([[live_w[m] * unit[x] for x in range(3)] for m in every], same)
        proj = [
            unit[0] * env[m][0] + unit[1] * env[m][1] + unit[2] * env[m][2] for m in every
        ]
        pre = [
            dot(
                deep[layer * CH:(layer + 1) * CH, :],
                three(jnp.concatenate([h[m], w[m] * proj[m]], axis=0)), 1, 0,
            )
            for m in every
        ]
        gate = [sigmoid(pre[m]) for m in every]
        saved.append((w, live_w, env, proj, pre, gate))
        h = [h[m] + pre[m] * gate[m] for m in every]
    z = [dot(ready(2), four(h[m]), 1, 0) for m in every]
    gate_z = [sigmoid(z[m]) for m in every]
    readout = sum(
        jnp.sum(lasts[m] * (z[m] * gate_z[m]), axis=0, keepdims=True) for m in every
    )

    def slope(pre, gate):
        return gate * (1.0 + pre * (1.0 - gate))

    weight_z = u * live
    one = jnp.where(count[0] > -1, 1.0, 0.0)
    dh = [
        dot(ready(5), four((lasts[m] * weight_z) * slope(z[m], gate_z[m])), 1, 0)
        for m in every
    ]
    dunit = [jnp.zeros((1, PAIRS), F32) for _ in range(3)]
    for layer in reversed(range(LAYERS)):
        w, live_w, env, proj, pre, gate = saved[layer]
        djoined = [
            dot(ready(6 + 2 * layer, 2 * CH), four(dh[m] * slope(pre[m], gate[m])), 1, 0)
            for m in every
        ]
        dq = [djoined[m][CH:] for m in every]
        dproj = [dq[m] * w[m] for m in every]
        dspread = same_sum([[dproj[m] * unit[x] for x in range(3)] for m in every], same)
        dw = []
        for m in every:
            back = unit[0] * dspread[m][0] + unit[1] * dspread[m][1] + unit[2] * dspread[m][2]
            dw.append(dq[m] * proj[m] + live * back)
        for x in range(3):
            dunit[x] = dunit[x] + jnp.sum(
                sum(dproj[m] * env[m][x] + live_w[m] * dspread[m][x] for m in every),
                axis=0, keepdims=True,
            )
        held = [dh[m] + one * djoined[m][:CH] for m in every]
        step = [dot(ready(3 + layer), four(dw[m]), 1, 0) for m in every]
        if layer:
            dh = [held[m] + one * step[m] for m in every]
    grad_basis = jnp.zeros((NB, PAIRS), F32)
    for m in every:
        slope0 = slope(pre0[m], gate0[m])
        dpre0 = (held[m] + one * step[m]) * slope0
        grad_basis = grad_basis + one * dot(ready(10, 2 * NB), four(dpre0), 1, 0)[0:NB]
    dr = jnp.sum(grad_basis * dbasis, axis=0, keepdims=True) + readout * live * du
    along = dunit[0] * unit[0] + dunit[1] * unit[1] + dunit[2] * unit[2]
    radial_part = dr - along * inverse
    for x in range(3):
        out[x:x + 1, :] = jnp.where(usable, dunit[x] * inverse + unit[x] * radial_part, 0.0)
    out[3:4, :] = neighbour.astype(F32)


def spread_rows(ids, rows, grads, lane_row):
    mask = iota((rows, PAIRS), 0) == ids
    full = jnp.concatenate([jnp.where(mask, grads[x], 0.0) for x in range(3)], axis=0)
    hi, lo = split2(full)
    lanes = (iota((LANES, PAIRS), 0) == lane_row).astype(F32).astype(BF16)
    both = dot(jnp.concatenate([hi, lo], axis=0), lanes, 1, 1)
    both = both[:3 * rows] + both[3 * rows:]
    return [both[x * rows:(x + 1) * rows] for x in range(3)]


def ghost_code(neighbour, source):
    ghost = jnp.maximum(neighbour - OWN, 0)
    apart = (ghost >> 9) ^ source
    code = [((apart >> k) & 1) + 2 * ((apart >> (k + 3)) & 1) for k in range(3)]
    return code, (ghost >> 7) & 3


def scatter_kernel(grad, core_grad, pairs, out, own):
    me = lax.axis_index("domain")
    core = me & 1
    out[...] = jnp.zeros(out.shape, F32)

    centre = pair_rows(pairs, 0)
    neighbour = pair_rows(pairs, 1)
    code, g = ghost_code(neighbour, me)
    ids = BINS + ((code[0] >> 1) + 2 * code[1] + 6 * code[2] - 1) * GS + g
    ids = jnp.where(neighbour < OWN, neighbour >> 7, jnp.where(code[0] == 1, -1, ids))
    grads = [grad[x:x + 1, :] for x in range(3)]
    far = spread_rows(ids, 96, grads, neighbour & 127)
    near = spread_rows(centre >> 7, BINS, grads, centre & 127)
    for x in range(3):
        own[x] = near[x] - far[x][0:BINS]
    for i, mask in enumerate([mask for mask in NEAR if not mask & 1][1:]):
        start = BINS + i * GS
        for x in range(3):
            row = core * 3 * GS + x * GS
            out[(me ^ mask) >> 1, pl.ds(row, GS), :] = -far[x][start:start + GS]

    neighbour = (0.25 * core_grad[3:4, :]).astype(I32)
    code, g = ghost_code(neighbour, me ^ 1)
    ids = (code[1] + 3 * code[2]) * GS + g
    ids = jnp.where((neighbour < OWN) | (code[0] != 1), -1, ids)
    grads = [core_grad[x:x + 1, :] for x in range(3)]
    far = spread_rows(ids, 48, grads, neighbour & 127)
    for i, mask in enumerate([mask for mask in NEAR if mask & 1]):
        for x in range(3):
            row = (1 - core) * 3 * GS + x * GS
            out[(me ^ 1 ^ mask) >> 1, pl.ds(row, GS), :] = -far[x][i * GS:(i + 1) * GS]


def finish_kernel(returned, lists, own, kind, half, vel_new, force_new):
    chips = NDOM // 2
    chosen = jnp.concatenate(
        [
            (jnp.broadcast_to(lists[r:r + 1, :], (BINS, chips)) == iota((BINS, chips), 0)).astype(F32)
            for r in range(2 * GS)
        ],
        axis=1,
    ).astype(BF16)
    mass = mass_of(kind[...])
    for x in range(3):
        data = jnp.concatenate(
            [
                returned[:, core * 3 * GS + x * GS + g, :]
                for g in range(GS) for core in range(2)
            ],
            axis=0,
        )
        hi, lo = split2(data)
        added = dot(chosen, hi, 1, 0) + dot(chosen, lo, 1, 0)
        force = (own[x] + added) * 0.25
        force_new[x] = force
        vel_new[x] = half[x] + 0.5 * TIME_STEP * force / mass


def call(kernel, name, shapes, args, specs=None, scratch=(), limit=32):
    out = tuple(jax.ShapeDtypeStruct(s, d) for s, d in shapes)
    return pl.pallas_call(
        kernel,
        name=name,
        out_shape=out,
        in_specs=specs or [VMEM] * len(args),
        out_specs=tuple(VMEM for _ in out),
        scratch_shapes=list(scratch),
        compiler_params=pltpu.CompilerParams(vmem_limit_bytes=limit * 1024 * 1024),
    )(*args)


ALONG_Y = [[g * GROUP + c + 2 * i for i in range(4)] for g in range(GROUP) for c in range(2)]
HIGH = [[g * GROUP + i for g in range(GROUP)] for i in range(GROUP)]
CHIPS = [[2 * i + c for i in range(NDOM // 2)] for c in range(2)]


def other_core(x):
    return lax.ppermute(x, "domain", [(i, i ^ 1) for i in range(NDOM)])


def on_device(
    positions, velocities, forces_old, species, swap_lists, ghost_lists, pair_lists, tile_counts,
    w_in, pair_embed, w_env, w_mid, w_out, w_last,
):
    turn = lambda x: jnp.transpose(x, (1, 0, 2))
    ghosts_of = jnp.transpose(ghost_lists, (0, 2, 1))
    loads = (turn(positions), turn(velocities), turn(forces_old), species, ghosts_of)
    (packed,) = call(
        start_kernel, "start", [((4, BINS, WIDE), F32)],
        loads + (turn(swap_lists),),
        [HBM] * len(loads) + [SMEM],
        [pltpu.VMEM(x.shape, x.dtype) for x in loads]
        + [pltpu.VMEM((LANES, LANES), F32), pltpu.SemaphoreType.DMA((len(loads),))],
        limit=60,
    )
    near = lax.all_to_all(packed, "domain", 0, 0, axis_index_groups=ALONG_Y, tiled=True)
    other = other_core(near)
    ghosts, places = call(
        ghost_kernel, "ghosts",
        [((GROUP, 4 * GS, HALF), F32), ((GROUP, LANES), I32)], (near, other),
    )
    far = lax.all_to_all(ghosts, "domain", 0, 0, axis_index_groups=HIGH, tiled=True)
    same, atoms, index, first, square, deep = call(
        pair_kernel, "pairs",
        [((PAIRS, PAIRS), BF16), ((8, PAIRS), F32), ((3, PAIRS), I32), ((2 * NB, LANES), F32),
         ((FIRST + 2 * NB, 4 * CH), BF16), ((2 * CH, 6 * CH), BF16)],
        (near, other, places, pair_lists, w_in, pair_embed, w_env,
         jnp.transpose(w_mid, (0, 1, 3, 2)), w_out),
    )
    (grad,) = call(
        force_kernel, "forces", [((4, PAIRS), F32)],
        (same, atoms, index, far, tile_counts, first, square, deep, w_last.reshape(CH, 1)),
        [VMEM] * 4 + [SMEM] + [VMEM] * 4,
    )
    grad = grad + lax.ppermute(grad, "member", [(i, i ^ 1) for i in range(4)])
    grad = grad + lax.ppermute(grad, "member", [(i, 3 - i) for i in range(4)])
    core_grad = other_core(grad)
    outgoing, own = call(
        scatter_kernel, "scatter",
        [((NDOM // 2, 6 * GS, LANES), F32), ((3, BINS, LANES), F32)],
        (grad, core_grad, pair_lists),
    )
    returned = lax.all_to_all(outgoing, "domain", 0, 0, axis_index_groups=CHIPS, tiled=True)
    pos_new, kind, half_new = call(
        own_kernel, "own",
        [((3, BINS, LANES), F32), ((BINS, LANES), F32), ((3, BINS, LANES), F32)],
        (near, other, places),
    )
    lists = ghost_lists[0].reshape(NDOM // 2, 2, GS).transpose(2, 1, 0).reshape(2 * GS, NDOM // 2)
    vel_new, force_new = call(
        finish_kernel, "finish",
        [((3, BINS, LANES), F32), ((3, BINS, LANES), F32)],
        (returned, lists, own, kind, half_new),
    )
    return turn(pos_new), turn(vel_new), turn(force_new)


def solution(mesh):
    return jax.shard_map(
        on_device,
        mesh=mesh,
        in_specs=(
            P("domain", None, None),
            P("domain", None, None),
            P("domain", None, None),
            P("domain", None),
            P("domain", None, None),
            P("domain", None, None),
            P("domain", None, None),
            P("domain"),
            P("member", None, None),
            P("member", None, None),
            P("member", None, None, None),
            P("member", None, None, None),
            P("member", None, None),
            P("member", None),
        ),
        out_specs=(P("domain", None, None), P("domain", None, None), P("domain", None, None)),
        check_vma=False,
    )
```

```python
import functools
import math

import jax
import jax.numpy as jnp
from jax import lax
from jax.experimental import pallas as pl
from jax.experimental.pallas import tpu as pltpu
from jax.sharding import PartitionSpec as P

TIME_STEP = 0.1
SOFTENING = 0.5
CUTOFF = 6.0
MASS_HYDROGEN = 1.008
MASS_OXYGEN = 15.999

NDOM = 64
GROUP = 8
BINS = 16
LANES = 128
TILES = 4
PAIRS = TILES * LANES
OWN = BINS * LANES
CH = 64
NB = 8
LAYERS = 2
LEVELS = 3
MOVE = 8
GS = 4


SPEC = 3 * LANES
HALF = 4 * LANES
LIST = 7 * LANES
WIDE = 8 * LANES

BACK = 6 * CH
FIRST = 10 * CH

F32 = jnp.float32
BF16 = jnp.bfloat16
I32 = jnp.int32

NEAR = []
for c2 in range(3):
    for c1 in range(3):
        for c0 in range(3):
            NEAR.append(
                (c0 & 1) | (c1 & 1) << 1 | (c2 & 1) << 2
                | (c0 >> 1) << 3 | (c1 >> 1) << 4 | (c2 >> 1) << 5
            )

VMEM = pl.BlockSpec(memory_space=pltpu.VMEM)
SMEM = pl.BlockSpec(memory_space=pltpu.SMEM)
HBM = pl.BlockSpec(memory_space=pltpu.HBM)


def iota(shape, dim):
    return lax.broadcasted_iota(I32, shape, dim)


def dot(a, b, ca, cb):
    return lax.dot_general(a, b, (((ca,), (cb,)), ((), ())), preferred_element_type=F32)


def split2(x):
    hi = x.astype(BF16)
    return hi, (x - hi.astype(F32)).astype(BF16)


def split3(x):
    hi = x.astype(BF16)
    rest = x - hi.astype(F32)
    mid = rest.astype(BF16)
    return hi, mid, (rest - mid.astype(F32)).astype(BF16)


def mass_of(kind):
    return jnp.where(kind == 1.0, MASS_OXYGEN, jnp.where(kind == 0.0, MASS_HYDROGEN, 1.0))


def low_of(k, me):
    return (k >> 2) | (((k & 3) ^ ((me >> 1) & 3)) << 1)


def place_of(low, me):
    return (((low ^ me) & 1) << 2) | (low >> 1)


def record(group, k):
    return group[k // 4], k % 4


def lists_toward(group, k, me):
    ref, y = record(group, k)
    rows = ref[y, MOVE:BINS, LIST:WIDE]
    return jnp.where((me & 1) == 0, rows, pltpu.roll(rows, LANES - GS, 1)).astype(I32)


def table(group, start, stop):
    return jnp.concatenate(
        [ref[:, :, start:stop].reshape(4 * BINS, stop - start) for ref in group], axis=0
    )


def slot_of(low, high):
    drop0 = low >> 1
    drop1 = (low & 1) | ((low >> 2) << 1)
    drop2 = low & 3
    return jnp.where((high & 1) != 0, drop0, jnp.where((high & 2) != 0, drop1, drop2))


def start_kernel(*refs):
    count = 5
    sources = refs[:count]
    swap, out = refs[count:count + 2]
    copies = refs[count + 2:2 * count + 2]
    turned, sems = refs[2 * count + 2:]
    moves = [
        pltpu.make_async_copy(sources[i], copies[i], sems.at[i]) for i in range(count)
    ]
    for move in moves:
        move.start()
    pos, vel, force, species, ghost = copies

    listed = jnp.zeros((MOVE, LANES), F32)
    row = iota((MOVE, LANES), 0)
    lane = iota((MOVE, LANES), 1)
    for level in range(LEVELS):
        for k in range(MOVE):
            listed = jnp.where(
                (row == k) & (lane == level), swap[level, 0, k].astype(F32), listed
            )
    turned[...] = jnp.zeros((LANES, LANES), F32)
    for move in moves:
        move.wait()

    turned[0:GS, 0:NDOM] = ghost[0].astype(F32)
    turned[...] = jnp.transpose(turned[...])
    kind = species[...].astype(F32)
    mass = mass_of(kind)
    drift = []
    half = []
    for x in range(3):
        kick = vel[x] + 0.5 * TIME_STEP * force[x] / mass
        half.append(kick)
        drift.append(pos[x] + TIME_STEP * kick)
    packed = jnp.concatenate(drift + [kind] + half, axis=1)
    for y in range(4):
        out[y, :, 0:LIST] = packed
        out[y, 0:MOVE, LIST:WIDE] = listed
        toward = [turned[pl.ds(2 * y + core, GROUP, stride=GROUP), :] for core in range(2)]
        out[y, MOVE:BINS, LIST:WIDE] = toward[0] + pltpu.roll(toward[1], GS, 1)


def final_places(group):
    lane = iota((MOVE, LANES), 1)
    dom = lane // BINS
    own_bin = lane % BINS
    total = lane
    for level in reversed(range(LEVELS)):
        mine = jnp.zeros((MOVE, LANES), I32)
        for s in range(GROUP):
            ref, y = record(group, s)
            column = ref[y, 0:MOVE, LIST:WIDE][:, level:level + 1].astype(I32)
            mine = jnp.where(dom == s, column, mine)
        bit = (4, 1, 2)[level]
        theirs = jnp.where(
            (dom & bit) != 0,
            pltpu.roll(mine, bit * BINS, 1),
            pltpu.roll(mine, LANES - bit * BINS, 1),
        )
        hit = mine == own_bin
        found = jnp.where(hit, (dom ^ bit) * BINS + theirs - lane, 0)
        source = lane + jnp.broadcast_to(jnp.sum(found, axis=0, keepdims=True), (MOVE, LANES))
        total = jnp.take_along_axis(source, total, axis=1)
    return total


def place_matrix(total):
    wide = jnp.broadcast_to(total[0:1, :], (LANES, LANES))
    return (iota((LANES, LANES), 0) == wide).astype(F32).astype(BF16)


def select_rows(chosen, data):
    hi, mid, lo = split3(data)
    return (dot(chosen, hi, 1, 0) + dot(chosen, mid, 1, 0)) + dot(chosen, lo, 1, 0)


def ghost_kernel(near, other, out, places):
    group = (near, other)
    me = lax.axis_index("domain")
    high_me = me // GROUP
    total = final_places(group)
    places[...] = total
    matrix = place_matrix(total)
    lane = iota((GROUP, LANES), 1)
    high = iota((GROUP, LANES), 0) ^ high_me
    rows = [[jnp.zeros((GROUP, LANES), jnp.bool_) for _ in range(GS)] for _ in range(4)]
    for s in range(GROUP):
        low = low_of(s, me)
        use = ((low & high) == 0) & (high != 0)
        slot = slot_of(low, high)
        lists = lists_toward(group, s, me)
        for g in range(GS):
            column = lists[:, g:g + 1]
            hit = (column + s * BINS == lane) & (column >= 0) & use
            for q in range(4):
                rows[q][g] = rows[q][g] | (hit & (slot == q))
    chosen = jnp.concatenate(
        [rows[q][g].astype(F32) for q in range(4) for g in range(GS)], axis=0
    ).astype(BF16)
    chosen = dot(chosen, matrix, 1, 1).astype(BF16)
    picked = select_rows(chosen, table(group, 0, HALF))
    for r in range(4 * GS):
        out[:, r, :] = picked[r * GROUP:(r + 1) * GROUP, :]


def own_kernel(near, other, places, pos_new, kind, half):
    group = (near, other)
    place_me = (lax.axis_index("domain") >> 1) & 3
    matrix = place_matrix(places[...])
    chosen = (iota((BINS, LANES), 1) == iota((BINS, LANES), 0) + place_me * BINS)
    chosen = dot(chosen.astype(F32).astype(BF16), matrix, 1, 1).astype(BF16)
    picked = select_rows(chosen, table(group, 0, LIST))
    kind[...] = picked[:, SPEC:HALF]
    for x in range(3):
        pos_new[x] = picked[:, x * LANES:(x + 1) * LANES]
        half[x] = picked[:, HALF + x * LANES:HALF + (x + 1) * LANES]


def take_row(table, index):
    parts = []
    for t in range(TILES):
        part = jnp.broadcast_to(index[:, t * LANES:(t + 1) * LANES], table.shape)
        parts.append(jnp.take_along_axis(table, part, axis=1)[0:1, :])
    return jnp.concatenate(parts, axis=1)


def pick(blocks, record, lane):
    columns = [[] for _ in range(4)]
    for t in range(TILES):
        cut = slice(t * LANES, (t + 1) * LANES)
        where_lane = jnp.broadcast_to(lane[:, cut], (8, LANES))
        where_bin = jnp.broadcast_to(record[:, cut], (8, LANES)) - iota((8, LANES), 0)
        sums = [jnp.zeros((8, LANES), F32) for _ in range(4)]
        for k, block in enumerate(blocks):
            hit = where_bin == 8 * k
            for x in range(4):
                got = jnp.take_along_axis(block(x), where_lane, axis=1)
                sums[x] = jnp.where(hit, got, sums[x])
        for x in range(4):
            columns[x].append(jnp.sum(sums[x], axis=0, keepdims=True))
    return [jnp.concatenate(c, axis=1) for c in columns]


def three(x):
    hi, lo = split2(x)
    return jnp.concatenate([hi, hi, lo], axis=0)


def mm_t(weight, x):
    hi, lo = split2(weight)
    return dot(jnp.concatenate([hi, lo, hi], axis=0), x, 0, 0)


def four(x):
    return jnp.concatenate([three(x), jnp.zeros(x.shape, BF16)], axis=0)


def left(weight):
    hi, lo = split2(weight)
    return jnp.concatenate([hi, lo, hi, jnp.zeros(hi.shape, BF16)], axis=1)


def turn_over(x):
    if x.shape[1] < LANES:
        x = jnp.concatenate([x, jnp.zeros((x.shape[0], LANES - x.shape[1]), F32)], axis=1)
    if x.shape[0] < LANES:
        x = jnp.concatenate([x, jnp.zeros((LANES - x.shape[0], LANES), F32)], axis=0)
    return jnp.transpose(x)


def sigmoid(x):
    return 1.0 / (1.0 + jnp.exp(-x))


def same_sum(parts, same):
    high = []
    low = []
    for part in parts:
        hi, lo = split2(jnp.concatenate(part, axis=0))
        high.append(hi)
        low.append(lo)
    both = dot(jnp.concatenate(high + low, axis=0), same, 1, 0)
    n = 3 * CH
    result = []
    for m in range(len(parts)):
        total = both[m * n:(m + 1) * n] + both[(len(parts) + m) * n:(len(parts) + m + 1) * n]
        result.append([total[x * CH:(x + 1) * CH] for x in range(3)])
    return result


def pair_rows(pairs, which):
    return jnp.concatenate([pairs[t, which:which + 1, :] for t in range(TILES)], axis=1)


def pair_kernel(
    near, other, places, pairs, w_in, pair_embed, w_env, w_mid_t, w_out,
    same, atoms, index, first, square, deep,
):
    first[...] = jnp.zeros(first.shape, F32)
    first[0:NB, 0:CH] = w_in[0]
    first[NB:NB + 4, 0:CH] = pair_embed[0]
    for k, weight in enumerate((w_env[0, 0], w_env[0, 1], w_out[0])):
        square[k * CH:(k + 1) * CH, :] = left(turn_over(weight)[0:CH, 0:CH])
        square[(3 + k) * CH:(4 + k) * CH, :] = left(weight)
    for layer in range(LAYERS):
        weight = w_mid_t[0, layer]
        start = BACK + layer * 2 * CH
        square[start:start + 2 * CH, :] = left(turn_over(weight)[:, 0:CH])
        hi, lo = split2(weight)
        deep[layer * CH:(layer + 1) * CH, :] = jnp.concatenate([hi, lo, hi], axis=1)
    square[FIRST:FIRST + 2 * NB, :] = left(first[:, 0:CH])

    group = (near, other)
    me = lax.axis_index("domain")
    low_me = me % GROUP
    high_me = me // GROUP
    place_me = low_me >> 1
    total = places[...]
    centre = pair_rows(pairs, 0)
    neighbour = pair_rows(pairs, 1)

    lane8 = iota((GROUP, LANES), 1)
    listed = jnp.zeros((GROUP, LANES), I32)
    for s in range(GROUP):
        rows = lists_toward(group, s, me)
        rows = pltpu.roll(rows, s * BINS, 1) if s else rows
        listed = jnp.where(lane8 // BINS == s, rows, listed)
    listed = jnp.where(iota((GROUP, LANES), 0) == high_me, listed, 0)
    listed = jnp.broadcast_to(jnp.sum(listed, axis=0, keepdims=True), (GROUP, LANES))
    local_place = (lane8 // BINS) * BINS + jnp.maximum(listed, 0)
    local_total = jnp.take_along_axis(total, local_place, axis=1)

    centre_bin = take_row(total, place_me * BINS + (centre >> 7))
    centre_lane = centre & 127
    ghost = neighbour - OWN
    is_own = ghost < 0
    p = jnp.maximum(ghost, 0) >> 9
    g = (jnp.maximum(ghost, 0) >> 7) & 3
    p_low = p & 7
    p_high = p >> 3
    own_bin = take_row(total, place_me * BINS + jnp.where(is_own, neighbour >> 7, 0))
    local_bin = take_row(local_total, place_of(p_low, me) * BINS + g)
    slot = slot_of(p_low ^ low_me, p_high ^ high_me) & 3
    is_far = (~is_own) & (p_high != high_me)
    near_bin = jnp.where(is_own, own_bin, jnp.where(is_far, -1, local_bin))
    neighbour_lane = neighbour & 127
    far_bin = jnp.where(is_far, p_high * BINS + slot * GS + g, -1)

    def piece(ref, s, half):
        return lambda x: ref[s, half * 8:(half + 1) * 8, x * LANES:(x + 1) * LANES]

    near_blocks = [piece(*record(group, s), half) for s in range(GROUP) for half in range(2)]
    xi = pick(near_blocks, centre_bin, centre_lane)
    xj = pick(near_blocks, near_bin, neighbour_lane)
    for x in range(4):
        atoms[x:x + 1, :] = xi[x]
        atoms[4 + x:5 + x, :] = xj[x]
    for r, values in enumerate((far_bin, neighbour_lane, neighbour)):
        index[r:r + 1, :] = values

    for a in range(TILES):
        wide = jnp.broadcast_to(centre[:, a * LANES:(a + 1) * LANES].astype(F32), (LANES, LANES))
        column = jnp.transpose(wide)
        same[a * LANES:(a + 1) * LANES, :] = (
            jnp.concatenate(
                [
                    (column == centre[:, b * LANES:(b + 1) * LANES].astype(F32)).astype(F32)
                    for b in range(TILES)
                ],
                axis=1,
            ).astype(BF16)
        )


def force_kernel(
    same_ref, atoms, index, far, count, first_weight, square, deep, last_column, out,
):
    def piece(h, half):
        return lambda x: far[h, half * 8:(half + 1) * 8, x * LANES:(x + 1) * LANES]

    same = same_ref[...]
    neighbour = index[2:3, :]
    blocks = [piece(h, half) for h in range(GROUP) for half in range(2)]
    xj = pick(blocks, index[0:1, :], index[1:2, :])
    xi = [atoms[x:x + 1, :] for x in range(4)]
    xj = [xj[x] + atoms[4 + x:5 + x, :] for x in range(4)]

    tile = iota((1, PAIRS), 1) // LANES
    delta = [xj[x] - xi[x] for x in range(3)]
    norm2 = delta[0] * delta[0] + delta[1] * delta[1] + delta[2] * delta[2]
    r = jnp.sqrt(norm2 + SOFTENING * SOFTENING)
    inverse = 1.0 / r
    unit = [delta[x] * inverse for x in range(3)]
    kind_i = xi[3].astype(I32)
    kind_j = xj[3].astype(I32)
    usable = (tile < count[0]) & (kind_i < 2) & (kind_j < 2) & (r < CUTOFF)
    live = usable.astype(F32)
    short = jnp.minimum(r, CUTOFF)
    s = short / CUTOFF
    s2 = s * s
    s5 = s2 * s2 * s
    s6 = s5 * s
    s7 = s6 * s
    u = 1.0 - 28.0 * s6 + 48.0 * s7 - 21.0 * s7 * s
    du = (-168.0 * s5 + 336.0 * s6 - 168.0 * s7) / CUTOFF
    wave = (iota((NB, PAIRS), 0) + 1).astype(F32) * (math.pi / CUTOFF)
    angle = wave * short
    sine = jnp.sin(angle)
    cosine = jnp.cos(angle)
    scale = math.sqrt(2.0 / CUTOFF)
    radial = scale * sine * inverse
    basis = radial * u
    dbasis = (scale * wave * cosine - radial) * inverse * u + radial * du

    pair_kind = jnp.clip(2 * kind_i + kind_j, 0, 3)
    onehot = (iota((NB, PAIRS), 0) == pair_kind).astype(F32)
    first = three(jnp.concatenate([basis, onehot], axis=0))
    every = range(1)

    def ready(k, rows=CH):
        return square[k * CH:k * CH + rows, :]

    lasts = [last_column[...]]
    pre0 = [mm_t(first_weight[:, 0:CH], first) for m in every]
    gate0 = [sigmoid(pre0[m]) for m in every]
    h = [pre0[m] * gate0[m] for m in every]
    saved = []
    for layer in range(LAYERS):
        w = [dot(ready(layer), four(h[m]), 1, 0) for m in every]
        live_w = [w[m] * live for m in every]
        env = same_sum([[live_w[m] * unit[x] for x in range(3)] for m in every], same)
        proj = [
            unit[0] * env[m][0] + unit[1] * env[m][1] + unit[2] * env[m][2] for m in every
        ]
        pre = [
            dot(
                deep[layer * CH:(layer + 1) * CH, :],
                three(jnp.concatenate([h[m], w[m] * proj[m]], axis=0)), 1, 0,
            )
            for m in every
        ]
        gate = [sigmoid(pre[m]) for m in every]
        saved.append((w, live_w, env, proj, pre, gate))
        h = [h[m] + pre[m] * gate[m] for m in every]
    z = [dot(ready(2), four(h[m]), 1, 0) for m in every]
    gate_z = [sigmoid(z[m]) for m in every]
    readout = sum(
        jnp.sum(lasts[m] * (z[m] * gate_z[m]), axis=0, keepdims=True) for m in every
    )

    def slope(pre, gate):
        return gate * (1.0 + pre * (1.0 - gate))

    weight_z = u * live
    one = jnp.where(count[0] > -1, 1.0, 0.0)
    dh = [
        dot(ready(5), four((lasts[m] * weight_z) * slope(z[m], gate_z[m])), 1, 0)
        for m in every
    ]
    dunit = [jnp.zeros((1, PAIRS), F32) for _ in range(3)]
    for layer in reversed(range(LAYERS)):
        w, live_w, env, proj, pre, gate = saved[layer]
        djoined = [
            dot(ready(6 + 2 * layer, 2 * CH), four(dh[m] * slope(pre[m], gate[m])), 1, 0)
            for m in every
        ]
        dq = [djoined[m][CH:] for m in every]
        dproj = [dq[m] * w[m] for m in every]
        dspread = same_sum([[dproj[m] * unit[x] for x in range(3)] for m in every], same)
        dw = []
        for m in every:
            back = unit[0] * dspread[m][0] + unit[1] * dspread[m][1] + unit[2] * dspread[m][2]
            dw.append(dq[m] * proj[m] + live * back)
        for x in range(3):
            dunit[x] = dunit[x] + jnp.sum(
                sum(dproj[m] * env[m][x] + live_w[m] * dspread[m][x] for m in every),
                axis=0, keepdims=True,
            )
        held = [dh[m] + one * djoined[m][:CH] for m in every]
        step = [dot(ready(3 + layer), four(dw[m]), 1, 0) for m in every]
        if layer:
            dh = [held[m] + one * step[m] for m in every]
    grad_basis = jnp.zeros((NB, PAIRS), F32)
    for m in every:
        slope0 = slope(pre0[m], gate0[m])
        dpre0 = (held[m] + one * step[m]) * slope0
        grad_basis = grad_basis + one * dot(ready(10, 2 * NB), four(dpre0), 1, 0)[0:NB]
    dr = jnp.sum(grad_basis * dbasis, axis=0, keepdims=True) + readout * live * du
    along = dunit[0] * unit[0] + dunit[1] * unit[1] + dunit[2] * unit[2]
    radial_part = dr - along * inverse
    for x in range(3):
        out[x:x + 1, :] = jnp.where(usable, dunit[x] * inverse + unit[x] * radial_part, 0.0)
    out[3:4, :] = neighbour.astype(F32)


def spread_rows(ids, rows, grads, lane_row):
    mask = iota((rows, PAIRS), 0) == ids
    full = jnp.concatenate([jnp.where(mask, grads[x], 0.0) for x in range(3)], axis=0)
    hi, lo = split2(full)
    lanes = (iota((LANES, PAIRS), 0) == lane_row).astype(F32).astype(BF16)
    both = dot(jnp.concatenate([hi, lo], axis=0), lanes, 1, 1)
    both = both[:3 * rows] + both[3 * rows:]
    return [both[x * rows:(x + 1) * rows] for x in range(3)]


def ghost_code(neighbour, source):
    ghost = jnp.maximum(neighbour - OWN, 0)
    apart = (ghost >> 9) ^ source
    code = [((apart >> k) & 1) + 2 * ((apart >> (k + 3)) & 1) for k in range(3)]
    return code, (ghost >> 7) & 3


def scatter_kernel(both, pairs, out, own):
    me = lax.axis_index("domain")
    core = me & 1
    out[...] = jnp.zeros(out.shape, F32)

    centre = pair_rows(pairs, 0)
    neighbour = pair_rows(pairs, 1)
    code, g = ghost_code(neighbour, me)
    ids = BINS + ((code[0] >> 1) + 2 * code[1] + 6 * code[2] - 1) * GS + g
    ids = jnp.where(neighbour < OWN, neighbour >> 7, jnp.where(code[0] == 1, -1, ids))
    grads = [both[0, x:x + 1, :] for x in range(3)]
    far = spread_rows(ids, 96, grads, neighbour & 127)
    near = spread_rows(centre >> 7, BINS, grads, centre & 127)
    for x in range(3):
        own[x] = near[x] - far[x][0:BINS]
    for i, mask in enumerate([mask for mask in NEAR if not mask & 1][1:]):
        start = BINS + i * GS
        for x in range(3):
            row = core * 3 * GS + x * GS
            out[(me ^ mask) >> 1, pl.ds(row, GS), :] = -far[x][start:start + GS]

    neighbour = (0.25 * both[1, 3:4, :]).astype(I32)
    code, g = ghost_code(neighbour, me ^ 1)
    ids = (code[1] + 3 * code[2]) * GS + g
    ids = jnp.where((neighbour < OWN) | (code[0] != 1), -1, ids)
    grads = [both[1, x:x + 1, :] for x in range(3)]
    far = spread_rows(ids, 48, grads, neighbour & 127)
    for i, mask in enumerate([mask for mask in NEAR if mask & 1]):
        for x in range(3):
            row = (1 - core) * 3 * GS + x * GS
            out[(me ^ 1 ^ mask) >> 1, pl.ds(row, GS), :] = -far[x][i * GS:(i + 1) * GS]


def finish_kernel(returned, lists, own, kind, half, vel_new, force_new):
    chips = NDOM // 2
    chosen = jnp.concatenate(
        [
            (jnp.broadcast_to(lists[r:r + 1, :], (BINS, chips)) == iota((BINS, chips), 0)).astype(F32)
            for r in range(2 * GS)
        ],
        axis=1,
    ).astype(BF16)
    mass = mass_of(kind[...])
    for x in range(3):
        data = jnp.concatenate(
            [
                returned[:, core * 3 * GS + x * GS + g, :]
                for g in range(GS) for core in range(2)
            ],
            axis=0,
        )
        hi, lo = split2(data)
        added = dot(chosen, hi, 1, 0) + dot(chosen, lo, 1, 0)
        force = (own[x] + added) * 0.25
        force_new[x] = force
        vel_new[x] = half[x] + 0.5 * TIME_STEP * force / mass


def call(kernel, name, shapes, args, specs=None, scratch=(), limit=32):
    out = tuple(jax.ShapeDtypeStruct(s, d) for s, d in shapes)
    return pl.pallas_call(
        kernel,
        name=name,
        out_shape=out,
        in_specs=specs or [VMEM] * len(args),
        out_specs=tuple(VMEM for _ in out),
        scratch_shapes=list(scratch),
        compiler_params=pltpu.CompilerParams(vmem_limit_bytes=limit * 1024 * 1024),
    )(*args)


ALONG_Y = [[g * GROUP + c + 2 * i for i in range(4)] for g in range(GROUP) for c in range(2)]
HIGH = [[g * GROUP + i for g in range(GROUP)] for i in range(GROUP)]
CHIPS = [[2 * i + c for i in range(NDOM // 2)] for c in range(2)]


def other_core(x):
    return lax.ppermute(x, "domain", [(i, i ^ 1) for i in range(NDOM)])


def on_device(
    positions, velocities, forces_old, species, swap_lists, ghost_lists, pair_lists, tile_counts,
    w_in, pair_embed, w_env, w_mid, w_out, w_last,
):
    turn = lambda x: jnp.transpose(x, (1, 0, 2))
    ghosts_of = jnp.transpose(ghost_lists, (0, 2, 1))
    loads = (turn(positions), turn(velocities), turn(forces_old), species, ghosts_of)
    (packed,) = call(
        start_kernel, "start", [((4, BINS, WIDE), F32)],
        loads + (turn(swap_lists),),
        [HBM] * len(loads) + [SMEM],
        [pltpu.VMEM(x.shape, x.dtype) for x in loads]
        + [pltpu.VMEM((LANES, LANES), F32), pltpu.SemaphoreType.DMA((len(loads),))],
        limit=60,
    )
    near = lax.all_to_all(packed, "domain", 0, 0, axis_index_groups=ALONG_Y, tiled=True)
    other = other_core(near)
    ghosts, places = call(
        ghost_kernel, "ghosts",
        [((GROUP, 4 * GS, HALF), F32), ((GROUP, LANES), I32)], (near, other),
    )
    far = lax.all_to_all(ghosts, "domain", 0, 0, axis_index_groups=HIGH, tiled=True)
    same, atoms, index, first, square, deep = call(
        pair_kernel, "pairs",
        [((PAIRS, PAIRS), BF16), ((8, PAIRS), F32), ((3, PAIRS), I32), ((2 * NB, LANES), F32),
         ((FIRST + 2 * NB, 4 * CH), BF16), ((2 * CH, 6 * CH), BF16)],
        (near, other, places, pair_lists, w_in, pair_embed, w_env,
         jnp.transpose(w_mid, (0, 1, 3, 2)), w_out),
    )
    (grad,) = call(
        force_kernel, "forces", [((4, PAIRS), F32)],
        (same, atoms, index, far, tile_counts, first, square, deep, w_last.reshape(CH, 1)),
        [VMEM] * 4 + [SMEM] + [VMEM] * 4,
    )
    both = jnp.stack([grad, other_core(grad)])
    both = both + lax.ppermute(both, "member", [(i, i ^ 1) for i in range(4)])
    both = both + lax.ppermute(both, "member", [(i, 3 - i) for i in range(4)])
    outgoing, own = call(
        scatter_kernel, "scatter",
        [((NDOM // 2, 6 * GS, LANES), F32), ((3, BINS, LANES), F32)],
        (both, pair_lists),
    )
    returned = lax.all_to_all(outgoing, "domain", 0, 0, axis_index_groups=CHIPS, tiled=True)
    pos_new, kind, half_new = call(
        own_kernel, "own",
        [((3, BINS, LANES), F32), ((BINS, LANES), F32), ((3, BINS, LANES), F32)],
        (near, other, places),
    )
    lists = ghost_lists[0].reshape(NDOM // 2, 2, GS).transpose(2, 1, 0).reshape(2 * GS, NDOM // 2)
    vel_new, force_new = call(
        finish_kernel, "finish",
        [((3, BINS, LANES), F32), ((3, BINS, LANES), F32)],
        (returned, lists, own, kind, half_new),
    )
    return turn(pos_new), turn(vel_new), turn(force_new)


def solution(mesh):
    return jax.shard_map(
        on_device,
        mesh=mesh,
        in_specs=(
            P("domain", None, None),
            P("domain", None, None),
            P("domain", None, None),
            P("domain", None),
            P("domain", None, None),
            P("domain", None, None),
            P("domain", None, None),
            P("domain"),
            P("member", None, None),
            P("member", None, None),
            P("member", None, None, None),
            P("member", None, None, None),
            P("member", None, None),
            P("member", None),
        ),
        out_specs=(P("domain", None, None), P("domain", None, None), P("domain", None, None)),
        check_vma=False,
    )
```

```python
import functools
import math

import jax
import jax.numpy as jnp
from jax import lax
from jax.experimental import pallas as pl
from jax.experimental.pallas import tpu as pltpu
from jax.sharding import PartitionSpec as P

TIME_STEP = 0.1
SOFTENING = 0.5
CUTOFF = 6.0
MASS_HYDROGEN = 1.008
MASS_OXYGEN = 15.999

NDOM = 64
GROUP = 8
BINS = 16
LANES = 128
TILES = 4
PAIRS = TILES * LANES
OWN = BINS * LANES
CH = 64
NB = 8
LAYERS = 2
LEVELS = 3
MOVE = 8
GS = 4


SPEC = 3 * LANES
HALF = 4 * LANES
LIST = 7 * LANES
WIDE = 8 * LANES

BACK = 6 * CH
FIRST = 10 * CH

F32 = jnp.float32
BF16 = jnp.bfloat16
I32 = jnp.int32

NEAR = []
for c2 in range(3):
    for c1 in range(3):
        for c0 in range(3):
            NEAR.append(
                (c0 & 1) | (c1 & 1) << 1 | (c2 & 1) << 2
                | (c0 >> 1) << 3 | (c1 >> 1) << 4 | (c2 >> 1) << 5
            )

VMEM = pl.BlockSpec(memory_space=pltpu.VMEM)
SMEM = pl.BlockSpec(memory_space=pltpu.SMEM)
HBM = pl.BlockSpec(memory_space=pltpu.HBM)


def iota(shape, dim):
    return lax.broadcasted_iota(I32, shape, dim)


def dot(a, b, ca, cb):
    return lax.dot_general(a, b, (((ca,), (cb,)), ((), ())), preferred_element_type=F32)


def split2(x):
    hi = x.astype(BF16)
    return hi, (x - hi.astype(F32)).astype(BF16)


def split3(x):
    hi = x.astype(BF16)
    rest = x - hi.astype(F32)
    mid = rest.astype(BF16)
    return hi, mid, (rest - mid.astype(F32)).astype(BF16)


def mass_of(kind):
    return jnp.where(kind == 1.0, MASS_OXYGEN, jnp.where(kind == 0.0, MASS_HYDROGEN, 1.0))


def low_of(k, me):
    return (k >> 2) | (((k & 3) ^ ((me >> 1) & 3)) << 1)


def place_of(low, me):
    return (((low ^ me) & 1) << 2) | (low >> 1)


def record(group, k):
    return group[k // 4], k % 4


def lists_toward(group, k, me):
    ref, y = record(group, k)
    rows = ref[y, MOVE:BINS, LIST:WIDE]
    return jnp.where((me & 1) == 0, rows, pltpu.roll(rows, LANES - GS, 1)).astype(I32)


def table(group, start, stop):
    return jnp.concatenate(
        [ref[:, :, start:stop].reshape(4 * BINS, stop - start) for ref in group], axis=0
    )


def slot_of(low, high):
    drop0 = low >> 1
    drop1 = (low & 1) | ((low >> 2) << 1)
    drop2 = low & 3
    return jnp.where((high & 1) != 0, drop0, jnp.where((high & 2) != 0, drop1, drop2))


def start_kernel(*refs):
    count = 5
    sources = refs[:count]
    swap, out = refs[count:count + 2]
    copies = refs[count + 2:2 * count + 2]
    turned, sems = refs[2 * count + 2:]
    moves = [
        pltpu.make_async_copy(sources[i], copies[i], sems.at[i]) for i in range(count)
    ]
    for move in moves:
        move.start()
    pos, vel, force, species, ghost = copies

    listed = jnp.zeros((MOVE, LANES), F32)
    row = iota((MOVE, LANES), 0)
    lane = iota((MOVE, LANES), 1)
    for level in range(LEVELS):
        for k in range(MOVE):
            listed = jnp.where(
                (row == k) & (lane == level), swap[level, 0, k].astype(F32), listed
            )
    turned[...] = jnp.zeros((LANES, LANES), F32)
    for move in moves:
        move.wait()

    turned[0:GS, 0:NDOM] = ghost[0].astype(F32)
    turned[...] = jnp.transpose(turned[...])
    kind = species[...].astype(F32)
    mass = mass_of(kind)
    drift = []
    half = []
    for x in range(3):
        kick = vel[x] + 0.5 * TIME_STEP * force[x] / mass
        half.append(kick)
        drift.append(pos[x] + TIME_STEP * kick)
    packed = jnp.concatenate(drift + [kind] + half, axis=1)
    for y in range(4):
        out[y, :, 0:LIST] = packed
        out[y, 0:MOVE, LIST:WIDE] = listed
        toward = [turned[pl.ds(2 * y + core, GROUP, stride=GROUP), :] for core in range(2)]
        out[y, MOVE:BINS, LIST:WIDE] = toward[0] + pltpu.roll(toward[1], GS, 1)


def final_places(group):
    lane = iota((MOVE, LANES), 1)
    dom = lane // BINS
    own_bin = lane % BINS
    total = lane
    for level in reversed(range(LEVELS)):
        mine = jnp.zeros((MOVE, LANES), I32)
        for s in range(GROUP):
            ref, y = record(group, s)
            column = ref[y, 0:MOVE, LIST:WIDE][:, level:level + 1].astype(I32)
            mine = jnp.where(dom == s, column, mine)
        bit = (4, 1, 2)[level]
        theirs = jnp.where(
            (dom & bit) != 0,
            pltpu.roll(mine, bit * BINS, 1),
            pltpu.roll(mine, LANES - bit * BINS, 1),
        )
        hit = mine == own_bin
        found = jnp.where(hit, (dom ^ bit) * BINS + theirs - lane, 0)
        source = lane + jnp.broadcast_to(jnp.sum(found, axis=0, keepdims=True), (MOVE, LANES))
        total = jnp.take_along_axis(source, total, axis=1)
    return total


def place_matrix(total):
    wide = jnp.broadcast_to(total[0:1, :], (LANES, LANES))
    return (iota((LANES, LANES), 0) == wide).astype(F32).astype(BF16)


def select_rows(chosen, data):
    chosen = jnp.concatenate([chosen] * 3, axis=1)
    return dot(chosen, jnp.concatenate(split3(data), axis=0), 1, 0)


def ghost_kernel(near, other, out, places):
    group = (near, other)
    me = lax.axis_index("domain")
    high_me = me // GROUP
    total = final_places(group)
    places[...] = total
    matrix = place_matrix(total)
    lane = iota((GROUP, LANES), 1)
    high = iota((GROUP, LANES), 0) ^ high_me
    rows = [[jnp.zeros((GROUP, LANES), jnp.bool_) for _ in range(GS)] for _ in range(4)]
    for s in range(GROUP):
        low = low_of(s, me)
        use = ((low & high) == 0) & (high != 0)
        slot = slot_of(low, high)
        lists = lists_toward(group, s, me)
        for g in range(GS):
            column = lists[:, g:g + 1]
            hit = (column + s * BINS == lane) & (column >= 0) & use
            for q in range(4):
                rows[q][g] = rows[q][g] | (hit & (slot == q))
    chosen = jnp.concatenate(
        [rows[q][g].astype(F32) for q in range(4) for g in range(GS)], axis=0
    ).astype(BF16)
    chosen = dot(chosen, matrix, 1, 1).astype(BF16)
    picked = select_rows(chosen, table(group, 0, HALF))
    for r in range(4 * GS):
        out[:, r, :] = picked[r * GROUP:(r + 1) * GROUP, :]


def own_kernel(near, other, places, pos_new, kind, half):
    group = (near, other)
    place_me = (lax.axis_index("domain") >> 1) & 3
    matrix = place_matrix(places[...])
    chosen = (iota((BINS, LANES), 1) == iota((BINS, LANES), 0) + place_me * BINS)
    chosen = dot(chosen.astype(F32).astype(BF16), matrix, 1, 1).astype(BF16)
    picked = select_rows(chosen, table(group, 0, LIST))
    kind[...] = picked[:, SPEC:HALF]
    for x in range(3):
        pos_new[x] = picked[:, x * LANES:(x + 1) * LANES]
        half[x] = picked[:, HALF + x * LANES:HALF + (x + 1) * LANES]


def take_row(table, index):
    parts = []
    for t in range(TILES):
        part = jnp.broadcast_to(index[:, t * LANES:(t + 1) * LANES], table.shape)
        parts.append(jnp.take_along_axis(table, part, axis=1)[0:1, :])
    return jnp.concatenate(parts, axis=1)


def pick(blocks, record, lane):
    columns = [[] for _ in range(4)]
    for t in range(TILES):
        cut = slice(t * LANES, (t + 1) * LANES)
        where_lane = jnp.broadcast_to(lane[:, cut], (8, LANES))
        where_bin = jnp.broadcast_to(record[:, cut], (8, LANES)) - iota((8, LANES), 0)
        sums = [jnp.zeros((8, LANES), F32) for _ in range(4)]
        for k, block in enumerate(blocks):
            hit = where_bin == 8 * k
            for x in range(4):
                got = jnp.take_along_axis(block(x), where_lane, axis=1)
                sums[x] = jnp.where(hit, got, sums[x])
        for x in range(4):
            columns[x].append(jnp.sum(sums[x], axis=0, keepdims=True))
    return [jnp.concatenate(c, axis=1) for c in columns]


def three(x):
    hi, lo = split2(x)
    return jnp.concatenate([hi, hi, lo], axis=0)


def mm_t(weight, x):
    hi, lo = split2(weight)
    return dot(jnp.concatenate([hi, lo, hi], axis=0), x, 0, 0)


def four(x):
    return jnp.concatenate([three(x), jnp.zeros(x.shape, BF16)], axis=0)


def left(weight):
    hi, lo = split2(weight)
    return jnp.concatenate([hi, lo, hi, jnp.zeros(hi.shape, BF16)], axis=1)


def turn_over(x):
    if x.shape[1] < LANES:
        x = jnp.concatenate([x, jnp.zeros((x.shape[0], LANES - x.shape[1]), F32)], axis=1)
    if x.shape[0] < LANES:
        x = jnp.concatenate([x, jnp.zeros((LANES - x.shape[0], LANES), F32)], axis=0)
    return jnp.transpose(x)


def sigmoid(x):
    return 1.0 / (1.0 + jnp.exp(-x))


def same_sum(parts, same):
    high = []
    low = []
    for part in parts:
        hi, lo = split2(jnp.concatenate(part, axis=0))
        high.append(hi)
        low.append(lo)
    both = dot(jnp.concatenate(high + low, axis=0), same, 1, 0)
    n = 3 * CH
    result = []
    for m in range(len(parts)):
        total = both[m * n:(m + 1) * n] + both[(len(parts) + m) * n:(len(parts) + m + 1) * n]
        result.append([total[x * CH:(x + 1) * CH] for x in range(3)])
    return result


def pair_rows(pairs, which):
    return jnp.concatenate([pairs[t, which:which + 1, :] for t in range(TILES)], axis=1)


def pair_kernel(
    near, other, places, pairs, w_in, pair_embed, w_env, w_mid_t, w_out,
    same, atoms, index, first, square, deep,
):
    first[...] = jnp.zeros(first.shape, F32)
    first[0:NB, 0:CH] = w_in[0]
    first[NB:NB + 4, 0:CH] = pair_embed[0]
    for k, weight in enumerate((w_env[0, 0], w_env[0, 1], w_out[0])):
        square[k * CH:(k + 1) * CH, :] = left(turn_over(weight)[0:CH, 0:CH])
        square[(3 + k) * CH:(4 + k) * CH, :] = left(weight)
    for layer in range(LAYERS):
        weight = w_mid_t[0, layer]
        start = BACK + layer * 2 * CH
        square[start:start + 2 * CH, :] = left(turn_over(weight)[:, 0:CH])
        hi, lo = split2(weight)
        deep[layer * CH:(layer + 1) * CH, :] = jnp.concatenate([hi, lo, hi], axis=1)
    square[FIRST:FIRST + 2 * NB, :] = left(first[:, 0:CH])

    group = (near, other)
    me = lax.axis_index("domain")
    low_me = me % GROUP
    high_me = me // GROUP
    place_me = low_me >> 1
    total = places[...]
    centre = pair_rows(pairs, 0)
    neighbour = pair_rows(pairs, 1)

    lane8 = iota((GROUP, LANES), 1)
    listed = jnp.zeros((GROUP, LANES), I32)
    for s in range(GROUP):
        rows = lists_toward(group, s, me)
        rows = pltpu.roll(rows, s * BINS, 1) if s else rows
        listed = jnp.where(lane8 // BINS == s, rows, listed)
    listed = jnp.where(iota((GROUP, LANES), 0) == high_me, listed, 0)
    listed = jnp.broadcast_to(jnp.sum(listed, axis=0, keepdims=True), (GROUP, LANES))
    local_place = (lane8 // BINS) * BINS + jnp.maximum(listed, 0)
    local_total = jnp.take_along_axis(total, local_place, axis=1)

    centre_bin = take_row(total, place_me * BINS + (centre >> 7))
    centre_lane = centre & 127
    ghost = neighbour - OWN
    is_own = ghost < 0
    p = jnp.maximum(ghost, 0) >> 9
    g = (jnp.maximum(ghost, 0) >> 7) & 3
    p_low = p & 7
    p_high = p >> 3
    own_bin = take_row(total, place_me * BINS + jnp.where(is_own, neighbour >> 7, 0))
    local_bin = take_row(local_total, place_of(p_low, me) * BINS + g)
    slot = slot_of(p_low ^ low_me, p_high ^ high_me) & 3
    is_far = (~is_own) & (p_high != high_me)
    near_bin = jnp.where(is_own, own_bin, jnp.where(is_far, -1, local_bin))
    neighbour_lane = neighbour & 127
    far_bin = jnp.where(is_far, p_high * BINS + slot * GS + g, -1)

    def piece(ref, s, half):
        return lambda x: ref[s, half * 8:(half + 1) * 8, x * LANES:(x + 1) * LANES]

    near_blocks = [piece(*record(group, s), half) for s in range(GROUP) for half in range(2)]
    xi = pick(near_blocks, centre_bin, centre_lane)
    xj = pick(near_blocks, near_bin, neighbour_lane)
    for x in range(4):
        atoms[x:x + 1, :] = xi[x]
        atoms[4 + x:5 + x, :] = xj[x]
    for r, values in enumerate((far_bin, neighbour_lane, neighbour)):
        index[r:r + 1, :] = values

    for a in range(TILES):
        wide = jnp.broadcast_to(centre[:, a * LANES:(a + 1) * LANES].astype(F32), (LANES, LANES))
        column = jnp.transpose(wide)
        same[a * LANES:(a + 1) * LANES, :] = (
            jnp.concatenate(
                [
                    (column == centre[:, b * LANES:(b + 1) * LANES].astype(F32)).astype(F32)
                    for b in range(TILES)
                ],
                axis=1,
            ).astype(BF16)
        )


def force_kernel(
    same_ref, atoms, index, far, count, first_weight, square, deep, last_column, out,
):
    def piece(h, half):
        return lambda x: far[h, half * 8:(half + 1) * 8, x * LANES:(x + 1) * LANES]

    same = same_ref[...]
    neighbour = index[2:3, :]
    blocks = [piece(h, half) for h in range(GROUP) for half in range(2)]
    xj = pick(blocks, index[0:1, :], index[1:2, :])
    xi = [atoms[x:x + 1, :] for x in range(4)]
    xj = [xj[x] + atoms[4 + x:5 + x, :] for x in range(4)]

    tile = iota((1, PAIRS), 1) // LANES
    delta = [xj[x] - xi[x] for x in range(3)]
    norm2 = delta[0] * delta[0] + delta[1] * delta[1] + delta[2] * delta[2]
    r = jnp.sqrt(norm2 + SOFTENING * SOFTENING)
    inverse = 1.0 / r
    unit = [delta[x] * inverse for x in range(3)]
    kind_i = xi[3].astype(I32)
    kind_j = xj[3].astype(I32)
    usable = (tile < count[0]) & (kind_i < 2) & (kind_j < 2) & (r < CUTOFF)
    live = usable.astype(F32)
    short = jnp.minimum(r, CUTOFF)
    s = short / CUTOFF
    s2 = s * s
    s5 = s2 * s2 * s
    s6 = s5 * s
    s7 = s6 * s
    u = 1.0 - 28.0 * s6 + 48.0 * s7 - 21.0 * s7 * s
    du = (-168.0 * s5 + 336.0 * s6 - 168.0 * s7) / CUTOFF
    wave = (iota((NB, PAIRS), 0) + 1).astype(F32) * (math.pi / CUTOFF)
    angle = wave * short
    sine = jnp.sin(angle)
    cosine = jnp.cos(angle)
    scale = math.sqrt(2.0 / CUTOFF)
    radial = scale * sine * inverse
    basis = radial * u
    dbasis = (scale * wave * cosine - radial) * inverse * u + radial * du

    pair_kind = jnp.clip(2 * kind_i + kind_j, 0, 3)
    onehot = (iota((NB, PAIRS), 0) == pair_kind).astype(F32)
    first = three(jnp.concatenate([basis, onehot], axis=0))
    every = range(1)

    def ready(k, rows=CH):
        return square[k * CH:k * CH + rows, :]

    lasts = [last_column[...]]
    pre0 = [mm_t(first_weight[:, 0:CH], first) for m in every]
    gate0 = [sigmoid(pre0[m]) for m in every]
    h = [pre0[m] * gate0[m] for m in every]
    saved = []
    for layer in range(LAYERS):
        w = [dot(ready(layer), four(h[m]), 1, 0) for m in every]
        live_w = [w[m] * live for m in every]
        env = same_sum([[live_w[m] * unit[x] for x in range(3)] for m in every], same)
        proj = [
            unit[0] * env[m][0] + unit[1] * env[m][1] + unit[2] * env[m][2] for m in every
        ]
        pre = [
            dot(
                deep[layer * CH:(layer + 1) * CH, :],
                three(jnp.concatenate([h[m], w[m] * proj[m]], axis=0)), 1, 0,
            )
            for m in every
        ]
        gate = [sigmoid(pre[m]) for m in every]
        saved.append((w, live_w, env, proj, pre, gate))
        h = [h[m] + pre[m] * gate[m] for m in every]
    z = [dot(ready(2), four(h[m]), 1, 0) for m in every]
    gate_z = [sigmoid(z[m]) for m in every]
    readout = sum(
        jnp.sum(lasts[m] * (z[m] * gate_z[m]), axis=0, keepdims=True) for m in every
    )

    def slope(pre, gate):
        return gate * (1.0 + pre * (1.0 - gate))

    weight_z = u * live
    one = jnp.where(count[0] > -1, 1.0, 0.0)
    dh = [
        dot(ready(5), four((lasts[m] * weight_z) * slope(z[m], gate_z[m])), 1, 0)
        for m in every
    ]
    dunit = [jnp.zeros((1, PAIRS), F32) for _ in range(3)]
    for layer in reversed(range(LAYERS)):
        w, live_w, env, proj, pre, gate = saved[layer]
        djoined = [
            dot(ready(6 + 2 * layer, 2 * CH), four(dh[m] * slope(pre[m], gate[m])), 1, 0)
            for m in every
        ]
        dq = [djoined[m][CH:] for m in every]
        dproj = [dq[m] * w[m] for m in every]
        dspread = same_sum([[dproj[m] * unit[x] for x in range(3)] for m in every], same)
        dw = []
        for m in every:
            back = unit[0] * dspread[m][0] + unit[1] * dspread[m][1] + unit[2] * dspread[m][2]
            dw.append(dq[m] * proj[m] + live * back)
        for x in range(3):
            dunit[x] = dunit[x] + jnp.sum(
                sum(dproj[m] * env[m][x] + live_w[m] * dspread[m][x] for m in every),
                axis=0, keepdims=True,
            )
        held = [dh[m] + one * djoined[m][:CH] for m in every]
        step = [dot(ready(3 + layer), four(dw[m]), 1, 0) for m in every]
        if layer:
            dh = [held[m] + one * step[m] for m in every]
    grad_basis = jnp.zeros((NB, PAIRS), F32)
    for m in every:
        slope0 = slope(pre0[m], gate0[m])
        dpre0 = (held[m] + one * step[m]) * slope0
        grad_basis = grad_basis + one * dot(ready(10, 2 * NB), four(dpre0), 1, 0)[0:NB]
    dr = jnp.sum(grad_basis * dbasis, axis=0, keepdims=True) + readout * live * du
    along = dunit[0] * unit[0] + dunit[1] * unit[1] + dunit[2] * unit[2]
    radial_part = dr - along * inverse
    for x in range(3):
        out[x:x + 1, :] = jnp.where(usable, dunit[x] * inverse + unit[x] * radial_part, 0.0)
    out[3:4, :] = neighbour.astype(F32)


def spread_rows(ids, rows, grads, lane_row):
    mask = iota((rows, PAIRS), 0) == ids
    full = jnp.concatenate([jnp.where(mask, grads[x], 0.0) for x in range(3)], axis=0)
    hi, lo = split2(full)
    lanes = (iota((LANES, PAIRS), 0) == lane_row).astype(F32).astype(BF16)
    both = dot(jnp.concatenate([hi, lo], axis=0), lanes, 1, 1)
    both = both[:3 * rows] + both[3 * rows:]
    return [both[x * rows:(x + 1) * rows] for x in range(3)]


def ghost_code(neighbour, source):
    ghost = jnp.maximum(neighbour - OWN, 0)
    apart = (ghost >> 9) ^ source
    code = [((apart >> k) & 1) + 2 * ((apart >> (k + 3)) & 1) for k in range(3)]
    return code, (ghost >> 7) & 3


def scatter_kernel(both, pairs, out, own):
    me = lax.axis_index("domain")
    out[...] = jnp.zeros(out.shape, F32)

    centre = pair_rows(pairs, 0)
    neighbour = pair_rows(pairs, 1)
    code, g = ghost_code(neighbour, me)
    ids = BINS + ((code[0] >> 1) + 2 * code[1] + 6 * code[2] - 1) * GS + g
    ids = jnp.where(neighbour < OWN, neighbour >> 7, jnp.where(code[0] == 1, -1, ids))
    grads = [both[0, x:x + 1, :] for x in range(3)]
    far = spread_rows(ids, 96, grads, neighbour & 127)
    near = spread_rows(centre >> 7, BINS, grads, centre & 127)
    for x in range(3):
        own[x] = near[x] - far[x][0:BINS]
    for i, mask in enumerate([mask for mask in NEAR if not mask & 1][1:]):
        start = BINS + i * GS
        for x in range(3):
            out[(me ^ mask) >> 1, x * GS:(x + 1) * GS, :] = -far[x][start:start + GS]

    neighbour = (0.25 * both[1, 3:4, :]).astype(I32)
    code, g = ghost_code(neighbour, me ^ 1)
    ids = (code[1] + 3 * code[2]) * GS + g
    ids = jnp.where((neighbour < OWN) | (code[0] != 1), -1, ids)
    grads = [both[1, x:x + 1, :] for x in range(3)]
    far = spread_rows(ids, 48, grads, neighbour & 127)
    for i, mask in enumerate([mask for mask in NEAR if mask & 1]):
        for x in range(3):
            row = (3 + x) * GS
            out[(me ^ 1 ^ mask) >> 1, row:row + GS, :] = -far[x][i * GS:(i + 1) * GS]


def finish_kernel(returned, lists, own, kind, half, vel_new, force_new):
    chips = NDOM // 2
    core = lax.axis_index("domain") & 1
    parts = []
    for g in range(GS):
        for apart in range(2):
            same, flip = 2 * g + apart, 2 * g + 1 - apart
            row = jnp.where(core == 0, lists[same:same + 1, :], lists[flip:flip + 1, :])
            hit = jnp.broadcast_to(row, (BINS, chips)) == iota((BINS, chips), 0)
            parts.append(hit.astype(F32))
    chosen = jnp.concatenate(parts, axis=1).astype(BF16)
    mass = mass_of(kind[...])
    for x in range(3):
        data = jnp.concatenate(
            [
                returned[:, apart * 3 * GS + x * GS + g, :]
                for g in range(GS) for apart in range(2)
            ],
            axis=0,
        )
        hi, lo = split2(data)
        added = dot(chosen, hi, 1, 0) + dot(chosen, lo, 1, 0)
        force = (own[x] + added) * 0.25
        force_new[x] = force
        vel_new[x] = half[x] + 0.5 * TIME_STEP * force / mass


def call(kernel, name, shapes, args, specs=None, scratch=(), limit=32):
    out = tuple(jax.ShapeDtypeStruct(s, d) for s, d in shapes)
    return pl.pallas_call(
        kernel,
        name=name,
        out_shape=out,
        in_specs=specs or [VMEM] * len(args),
        out_specs=tuple(VMEM for _ in out),
        scratch_shapes=list(scratch),
        compiler_params=pltpu.CompilerParams(vmem_limit_bytes=limit * 1024 * 1024),
    )(*args)


ALONG_Y = [[g * GROUP + c + 2 * i for i in range(4)] for g in range(GROUP) for c in range(2)]
HIGH = [[g * GROUP + i for g in range(GROUP)] for i in range(GROUP)]
CHIPS = [[2 * i + c for i in range(NDOM // 2)] for c in range(2)]


def other_core(x):
    return lax.ppermute(x, "domain", [(i, i ^ 1) for i in range(NDOM)])


def on_device(
    positions, velocities, forces_old, species, swap_lists, ghost_lists, pair_lists, tile_counts,
    w_in, pair_embed, w_env, w_mid, w_out, w_last,
):
    turn = lambda x: jnp.transpose(x, (1, 0, 2))
    ghosts_of = jnp.transpose(ghost_lists, (0, 2, 1))
    loads = (turn(positions), turn(velocities), turn(forces_old), species, ghosts_of)
    (packed,) = call(
        start_kernel, "start", [((4, BINS, WIDE), F32)],
        loads + (turn(swap_lists),),
        [HBM] * len(loads) + [SMEM],
        [pltpu.VMEM(x.shape, x.dtype) for x in loads]
        + [pltpu.VMEM((LANES, LANES), F32), pltpu.SemaphoreType.DMA((len(loads),))],
        limit=60,
    )
    near = lax.all_to_all(packed, "domain", 0, 0, axis_index_groups=ALONG_Y, tiled=True)
    other = other_core(near)
    ghosts, places = call(
        ghost_kernel, "ghosts",
        [((GROUP, 4 * GS, HALF), F32), ((GROUP, LANES), I32)], (near, other),
    )
    far = lax.all_to_all(ghosts, "domain", 0, 0, axis_index_groups=HIGH, tiled=True)
    same, atoms, index, first, square, deep = call(
        pair_kernel, "pairs",
        [((PAIRS, PAIRS), BF16), ((8, PAIRS), F32), ((3, PAIRS), I32), ((2 * NB, LANES), F32),
         ((FIRST + 2 * NB, 4 * CH), BF16), ((2 * CH, 6 * CH), BF16)],
        (near, other, places, pair_lists, w_in, pair_embed, w_env,
         jnp.transpose(w_mid, (0, 1, 3, 2)), w_out),
    )
    (grad,) = call(
        force_kernel, "forces", [((4, PAIRS), F32)],
        (same, atoms, index, far, tile_counts, first, square, deep, w_last.reshape(CH, 1)),
        [VMEM] * 4 + [SMEM] + [VMEM] * 4,
    )
    both = jnp.stack([grad, other_core(grad)])
    both = both + lax.ppermute(both, "member", [(i, i ^ 1) for i in range(4)])
    both = both + lax.ppermute(both, "member", [(i, 3 - i) for i in range(4)])
    outgoing, own = call(
        scatter_kernel, "scatter",
        [((NDOM // 2, 6 * GS, LANES), F32), ((3, BINS, LANES), F32)],
        (both, pair_lists),
    )
    returned = lax.all_to_all(outgoing, "domain", 0, 0, axis_index_groups=CHIPS, tiled=True)
    pos_new, kind, half_new = call(
        own_kernel, "own",
        [((3, BINS, LANES), F32), ((BINS, LANES), F32), ((3, BINS, LANES), F32)],
        (near, other, places),
    )
    lists = ghost_lists[0].reshape(NDOM // 2, 2, GS).transpose(2, 1, 0).reshape(2 * GS, NDOM // 2)
    vel_new, force_new = call(
        finish_kernel, "finish",
        [((3, BINS, LANES), F32), ((3, BINS, LANES), F32)],
        (returned, lists, own, kind, half_new),
    )
    return turn(pos_new), turn(vel_new), turn(force_new)


def solution(mesh):
    return jax.shard_map(
        on_device,
        mesh=mesh,
        in_specs=(
            P("domain", None, None),
            P("domain", None, None),
            P("domain", None, None),
            P("domain", None),
            P("domain", None, None),
            P("domain", None, None),
            P("domain", None, None),
            P("domain"),
            P("member", None, None),
            P("member", None, None),
            P("member", None, None, None),
            P("member", None, None, None),
            P("member", None, None),
            P("member", None),
        ),
        out_specs=(P("domain", None, None), P("domain", None, None), P("domain", None, None)),
        check_vma=False,
    )
```
